32 devices in a mesh: seq: 8 (over y, x, core), row: 4 (over z).
Axes of the slice: x: 2, y: 2, z: 4, core: 2. Of those that a mesh axis runs over, the one named last changes fastest.
Arguments:
- hidden: bfloat16 [4, 1024, 768], P('row', 'seq'), may hold values from -6 to 6
- segments: int32 [4, 1024], P('row', 'seq'), may hold values from 0 to 2, as said below
- rel_embed: bfloat16 [512, 768], replicated, may hold values from -6 to 6
- query_weight: bfloat16 [768, 768], replicated, may hold values from -0.3125 to 0.3125
- key_weight: bfloat16 [768, 768], replicated, may hold values from -0.3125 to 0.3125
- value_weight: bfloat16 [768, 768], replicated, may hold values from -0.21875 to 0.21875
- output_weight: bfloat16 [768, 768], replicated, may hold values from -1.75 to 1.75
- up_weight: bfloat16 [768, 3072], replicated, may hold values from -0.21875 to 0.21875
- down_weight: bfloat16 [3072, 768], replicated, may hold values from -0.109375 to 0.109375
- norm1_gain: float32 [768], replicated, may hold values from 0.5 to 1.5
- norm1_bias: float32 [768], replicated, may hold values from -1 to 1
- norm2_gain: float32 [768], replicated, may hold values from 0.5 to 1.5
- norm2_bias: float32 [768], replicated, may hold values from -1 to 1
- cotangent: bfloat16 [4, 1024, 768], P('row', 'seq'), may hold values from -6 to 6
Outputs:
- output: bfloat16 [4, 1024, 768], P('row', 'seq')
- grad_input: bfloat16 [4, 1024, 768], P('row', 'seq')
- grad_query_weight: float32 [768, 768], P('row')
- grad_key_weight: float32 [768, 768], P('row')
- grad_value_weight: float32 [768, 768], P('row')
- grad_output_weight: float32 [768, 768], P('row')
- grad_up_weight: float32 [768, 3072], P('row')
- grad_down_weight: float32 [3072, 768], P('row')
- grad_norm1_gain: float32 [768], P('row')
- grad_norm1_bias: float32 [768], P('row')
- grad_norm2_gain: float32 [768], P('row')
- grad_norm2_bias: float32 [768], P('row')
- grad_relative: float32 [512, 768], replicated
The draws below stay inside these ranges and needn't reach their ends.
Inputs may be any that keep to these rules, and one draw needn't show every extreme that they name: `segments`: along each row of 1024 slots the ids never fall and take the values 0, 1 and 2; document 1 begins within the row's first 128 slots and ends within its last 128 slots.
All inputs are finite; a program needn't handle non-finite values.
Results may differ from the reference program's by a relative error of at most 0.024.
Values may be sent and summed in bfloat16 or wider, within the bound.
No kernel may reach another device: no remote copies, remote signals or barrier semaphores. Data moves between devices by JAX's collectives and lax.ppermute only.
A program may use at most 256 MiB of HBM per device.

```python
import math
import jax
import jax.numpy as jnp
from jax import lax

D = 768
HEADS = 12
HEAD_DIM = 64
FF = 3072
SPAN = 256
TOK_DEV = 128
LEN = 1024
ROWS = 4


def draw_segments(key, part):
    key = jax.random.fold_in(key, 11)
    first_key, second_key = jax.random.split(key)
    opening = jax.random.randint(first_key, (ROWS, 1), 1, TOK_DEV)
    closing = LEN - jax.random.randint(second_key, (ROWS, 1), 1, TOK_DEV)
    places = jnp.arange(LEN, dtype=jnp.int32)[None, :]
    return (places >= opening).astype(jnp.int32) + (places >= closing).astype(jnp.int32)


def shard_levels(rng, dims, cuts, least, largest):
    def one(axis_at, blocks):
        heights = jax.random.uniform(jax.random.fold_in(jax.random.fold_in(rng, 6), axis_at), (blocks,), jnp.float32, least / len(cuts), largest / len(cuts))
        return jnp.repeat(jnp.exp(heights), dims[axis_at] // blocks).reshape((-1,) + (1,) * (len(dims) - axis_at - 1))

    level = one(*cuts[0])
    for cut in cuts[1:]:
        level = level * one(*cut)
    return level


def bell_draw(rng, dims, scale, most, cuts=(), kind=jnp.bfloat16):
    values = scale * jax.random.normal(rng, dims, jnp.float32)
    if cuts:
        values = values * shard_levels(rng, dims, cuts, -0.22, 0.18)
    return jnp.clip(values, -most, most).astype(kind)


def setup_inputs(seed: int = 0) -> dict:
    key_of = jax.random.split(jax.random.key(seed), 15)
    return {
        "hidden": bell_draw(key_of[0], (ROWS, LEN, D), 1.0, 6.0, ((0, 4), (1, 8))),
        "segments": draw_segments(jax.random.fold_in(key_of[14], 71), 0),
        "rel_embed": bell_draw(key_of[2], (2 * SPAN, D), 1.0, 6.0),
        "query_weight": bell_draw(key_of[3], (D, D), (D // 2) ** -0.5, 0.3125),
        "key_weight": bell_draw(key_of[4], (D, D), (D // 2) ** -0.5, 0.3125),
        "value_weight": bell_draw(key_of[5], (D, D), D ** -0.5, 0.21875),
        "output_weight": bell_draw(key_of[6], (D, D), (max(D // 64, 1)) ** -0.5, 1.75),
        "up_weight": bell_draw(key_of[7], (D, FF), D ** -0.5, 0.21875),
        "down_weight": bell_draw(key_of[8], (FF, D), FF ** -0.5, 0.109375),
        "norm1_gain": jnp.clip(1.0 + 0.1 * jax.random.normal(key_of[9], (D,), jnp.float32), 0.5, 1.5),
        "norm1_bias": bell_draw(key_of[10], (D,), 0.2, 1.0, (), jnp.float32),
        "norm2_gain": jnp.clip(1.0 + 0.1 * jax.random.normal(key_of[11], (D,), jnp.float32), 0.5, 1.5),
        "norm2_bias": bell_draw(key_of[12], (D,), 0.2, 1.0, (), jnp.float32),
        "cotangent": bell_draw(key_of[13], (ROWS, LEN, D), 1.0, 6.0, ((0, 4), (1, 8))),
    }


@jax.custom_vjp
def low(v):
    return lax.optimization_barrier(v.astype(jnp.bfloat16)).astype(jnp.float32)

@jax.custom_vjp
def low_back(v):
    return v

def low_keep(v):
    return (low(v), None)

def low_pass(kept, grad):
    return (grad,)

def back_keep(v):
    return (v, None)

def back_low(kept, grad):
    return (low(grad),)
low.defvjp(low_keep, low_pass)
low_back.defvjp(back_keep, back_low)
highest = lax.Precision.HIGHEST
epsilon = 1e-07
masked_value = -1e+30

def matmul(left, right):
    return jnp.dot(left, right, precision=highest)

def layer_norm(value, gain, shift):
    center = value - lax.optimization_barrier(jnp.mean(value, axis=-1, keepdims=True))
    spread = lax.optimization_barrier(jnp.mean(center * center, axis=-1, keepdims=True))
    return center * lax.rsqrt(spread + epsilon) * gain + shift

def attend_row(queries, keys, values, segs, query_rel, key_rel):
    block = math.gcd(LEN, 512)
    places = jnp.arange(LEN, dtype=jnp.int32)
    scale = 1.0 / math.sqrt(3.0 * HEAD_DIM)
    p2c_table = jnp.einsum('jhe,phe->hjp', keys, query_rel, precision=highest)

    def one_block(start):
        query_blk = lax.dynamic_slice_in_dim(queries, start, block, 0)
        pos_q = start + jnp.arange(block, dtype=jnp.int32)
        seg_q = lax.dynamic_slice_in_dim(segs, start, block, 0)
        direct = jnp.einsum('ihe,jhe->hij', query_blk, keys, precision=highest)
        c2p_table = jnp.einsum('ihe,phe->hip', query_blk, key_rel, precision=highest)
        fwd_index = jnp.clip(pos_q[:, None] - places[None, :], -SPAN, SPAN - 1) + SPAN
        c2p = jnp.take_along_axis(c2p_table, jnp.broadcast_to(fwd_index[None], (HEADS, block, LEN)), axis=2)
        back_index = jnp.clip(places[:, None] - pos_q[None, :], -SPAN, SPAN - 1) + SPAN
        p2c = jnp.take_along_axis(p2c_table, jnp.broadcast_to(back_index[None], (HEADS, LEN, block)), axis=2)
        logits = low_back((direct + c2p + jnp.transpose(p2c, (0, 2, 1))) * scale)
        allowed = (seg_q[:, None] == segs[None, :])[None]
        masked = jnp.where(allowed, logits, masked_value)
        shift = lax.optimization_barrier(jnp.max(masked, axis=2, keepdims=True))
        weights = jnp.exp(masked - shift)
        probs = weights / lax.optimization_barrier(jnp.sum(weights, axis=2, keepdims=True))
        return jnp.einsum('hij,jhe->ihe', low(probs), values, precision=highest)
    starts = block * jnp.arange(LEN // block, dtype=jnp.int32)
    return lax.map(jax.checkpoint(one_block), starts).reshape(LEN, D)

def reference(hidden, segments, rel_embed, query_weight, key_weight, value_weight, output_weight, up_weight, down_weight, norm1_gain, norm1_bias, norm2_gain, norm2_bias, cotangent):

    def forward(hidden_f, rel_f, w_query, w_key, w_value, w_output, w_up, w_down, gain_one, bias_one, gain_two, bias_two):
        query_rel = low_back(low(matmul(rel_f, w_query))).reshape(2 * SPAN, HEADS, HEAD_DIM)
        key_rel = low_back(low(matmul(rel_f, w_key))).reshape(2 * SPAN, HEADS, HEAD_DIM)

        def one_row(item):
            row_in, segs = item
            queries = low_back(low(matmul(row_in, w_query))).reshape(LEN, HEADS, HEAD_DIM)
            keys = low_back(low(matmul(row_in, w_key))).reshape(LEN, HEADS, HEAD_DIM)
            values = low_back(low(matmul(row_in, w_value))).reshape(LEN, HEADS, HEAD_DIM)
            context = low_back(low(attend_row(queries, keys, values, segs, query_rel, key_rel)))
            attn_out = low_back(matmul(context, w_output))
            normed_one = layer_norm(row_in + attn_out, gain_one, bias_one)
            inner = low_back(matmul(low(normed_one), w_up))
            active = low(jax.nn.gelu(inner, approximate=False))
            branch = low_back(matmul(active, w_down))
            return layer_norm(normed_one + branch, gain_two, bias_two)
        return lax.map(jax.checkpoint(one_row), (hidden_f, segments))
    primals = (hidden.astype(jnp.float32), rel_embed.astype(jnp.float32), query_weight.astype(jnp.float32), key_weight.astype(jnp.float32), value_weight.astype(jnp.float32), output_weight.astype(jnp.float32), up_weight.astype(jnp.float32), down_weight.astype(jnp.float32), norm1_gain.astype(jnp.float32), norm1_bias.astype(jnp.float32), norm2_gain.astype(jnp.float32), norm2_bias.astype(jnp.float32))
    result, pullback = jax.vjp(forward, *primals)
    grads = pullback(cotangent.astype(jnp.float32))
    return (result.astype(jnp.bfloat16), grads[0].astype(jnp.bfloat16), grads[2], grads[3], grads[4], grads[5], grads[6], grads[7], grads[8], grads[9], grads[10], grads[11], grads[1])
```

```python
import functools, math
import jax, jax.numpy as jnp
from jax import lax
from jax.experimental import pallas as pl
from jax.experimental.pallas import tpu as pltpu
from jax.sharding import PartitionSpec as P

BLK = 128
PAIR = 128
NT = (((1,), (1,)), ((), ()))
NN = (((1,), (0,)), ((), ()))
TN = (((0,), (0,)), ((), ()))
bf16 = jnp.bfloat16
f32 = jnp.float32


def dot(a, b, form):
    return lax.dot_general(a, b, form, preferred_element_type=f32)


def half_masks(x):
    lane = lax.broadcasted_iota(jnp.int32, x.shape, 1)
    low = lane < PAIR // 2
    zero = jnp.zeros_like(x)
    return jnp.where(low, x, zero), jnp.where(low, zero, x)


def join_heads(stacked, rows):
    lane = lax.broadcasted_iota(jnp.int32, (rows, PAIR), 1)
    return jnp.where(lane < PAIR // 2, stacked[:rows], stacked[rows:])


def fill_scores(own_ref, all_ref, near_ref, far_ref, s_ref, length):
    wide = length + BLK
    own = jnp.concatenate(half_masks(own_ref[...]), axis=0)
    ext = dot(own, near_ref[...], NT)
    for h in range(2):
        moved = pltpu.roll(ext[h * BLK:(h + 1) * BLK], wide - (BLK - 1), 1, stride=1, stride_axis=0)
        s_ref[h] = moved[:, :length]
    for c in range(length // BLK):
        cols = slice(c * BLK, (c + 1) * BLK)
        blk = all_ref[cols, :]
        both = jnp.concatenate(half_masks(blk), axis=0)
        start = length - BLK - BLK * c
        win = far_ref[start:start + 2 * BLK, :]
        back = dot(both, win, NT)
        direct = dot(own, blk, NT)
        for h in range(2):
            rows = slice(h * BLK, (h + 1) * BLK)
            moved = pltpu.roll(back[rows], BLK + 1, 1, stride=1, stride_axis=0)[:, :BLK]
            s_ref[h, :, cols] += direct[rows] + moved.T


def forward_kernel(scale, length, q_ref, k_ref, v_ref, near_ref, far_ref, segq_ref, segk_ref,
                   p_ref, ctx_ref, lse_ref, s_ref):
    fill_scores(q_ref, k_ref, near_ref, far_ref, s_ref, length)
    allowed = segq_ref[...] == segk_ref[...]
    stats = []
    for h in range(2):
        logits = jnp.where(allowed, s_ref[h] * scale, -1e30)
        best = jnp.max(logits, axis=1, keepdims=True)
        weights = jnp.exp(logits - best)
        total = jnp.sum(weights, axis=1, keepdims=True)
        p_ref[h] = (weights * (1.0 / total)).astype(bf16)
        stats.append(best + jnp.log(total))
    stacked = jnp.concatenate([p_ref[0], p_ref[1]], axis=0)
    ctx_ref[...] = join_heads(dot(stacked, v_ref[...], NN), BLK)
    lane = lax.broadcasted_iota(jnp.int32, (BLK, BLK), 1)
    tile = jnp.where(lane == 0, stats[0], stats[1])
    lse_ref[0] = tile.T[:8]


def other_probs_kernel(scale, length, k_ref, q_ref, near_ref, far_ref, segk_ref, segq_ref, lse_ref, p_ref, s_ref):
    fill_scores(k_ref, q_ref, near_ref, far_ref, s_ref, length)
    allowed = segk_ref[...] == segq_ref[...]
    for h in range(2):
        logits = s_ref[h] * scale - lse_ref[0, h:h + 1, :]
        p_ref[h] = jnp.where(allowed, jnp.exp(logits), 0.0).astype(bf16)


def flip_matrix():
    r = lax.broadcasted_iota(jnp.int32, (BLK, BLK), 0)
    c = lax.broadcasted_iota(jnp.int32, (BLK, BLK), 1)
    return jnp.where(r + c == BLK - 1, 1.0, 0.0).astype(bf16)


def grads_tail(scale, length, ds_refs, own_ref, all_ref, near_ref, wide_ref, down_ref):
    wide = length + BLK
    flip = flip_matrix()
    for h in range(2):
        back = dot(flip, ds_refs[h], NN)
        down_ref[h * BLK:(h + 1) * BLK, :] = back.astype(bf16)
        padded = jnp.concatenate([back, jnp.zeros((BLK, BLK), f32)], axis=1)
        wide_ref[h * BLK:(h + 1) * BLK, :] = pltpu.roll(padded, 0, 1, stride=1, stride_axis=0).astype(bf16)
    own_grad = dot(down_ref[...], all_ref[...], NN) + dot(wide_ref[...], near_ref[...], NN)
    own_grad = (join_heads(own_grad, BLK) * scale).astype(bf16)
    own_grad = dot(flip, own_grad, NN).astype(bf16)
    own = dot(flip, own_ref[...], NN).astype(bf16)
    own = jnp.concatenate(half_masks(own), axis=0)
    near_grad = dot(own, wide_ref[...], TN) * scale
    return own_grad, near_grad


def query_grad_kernel(scale, length, p_ref, dctx_ref, ctx_ref, v_ref, q_ref, k_ref, near_ref,
                      dq_ref, dnear_ref, ds_ref, wide_ref, down_ref):
    dctx = jnp.concatenate(half_masks(dctx_ref[...]), axis=0)
    dprob = dot(dctx, v_ref[...], NT)
    ctx = ctx_ref[...]
    for h in range(2):
        rows = slice(h * BLK, (h + 1) * BLK)
        row_dot = jnp.sum(dctx[rows].astype(f32) * ctx, axis=1, keepdims=True)
        ds_ref[h] = (p_ref[h].astype(f32) * (dprob[rows] - row_dot)).astype(bf16)
    dq, dnear = grads_tail(scale, length, ds_ref, q_ref, k_ref, near_ref, wide_ref, down_ref)
    dq_ref[...] = dq
    dnear_ref[...] = dnear.astype(dnear_ref.dtype)


def key_grad_kernel(scale, length, p_ref, v_ref, dctx_ref, rdot_ref, k_ref, q_ref, near_ref,
                    dk_ref, dv_ref, dnear_ref, ds_ref, wide_ref, down_ref):
    vals = jnp.concatenate(half_masks(v_ref[...]), axis=0)
    dctx = dctx_ref[...]
    dprob = dot(vals, dctx, NT)
    for h in range(2):
        rows = slice(h * BLK, (h + 1) * BLK)
        ds_ref[h] = (p_ref[h].astype(f32) * (dprob[rows] - rdot_ref[0, h:h + 1, :])).astype(bf16)
    stacked = jnp.concatenate([p_ref[0], p_ref[1]], axis=0)
    dv_ref[...] = join_heads(dot(stacked, dctx, NN), BLK).astype(bf16)
    dk, dnear = grads_tail(scale, length, ds_ref, k_ref, q_ref, near_ref, wide_ref, down_ref)
    dk_ref[...] = dk
    dnear_ref[...] = dnear.astype(dnear_ref.dtype)


def col(rows):
    return pl.BlockSpec((rows, PAIR), lambda p: (0, p))


def full(shape):
    return pl.BlockSpec(shape, lambda p: (0,) * len(shape))


def params():
    return pltpu.CompilerParams(vmem_limit_bytes=56 * 1024 * 1024)


def forward_attention(q, k, v, near, far, seg_q, seg_k, scale):
    length, width = k.shape
    pairs = width // PAIR
    wide = length + BLK
    return pl.pallas_call(
        functools.partial(forward_kernel, scale, length),
        grid=(pairs,),
        in_specs=[col(BLK), col(length), col(length), col(wide), col(wide), full((BLK, 1)), full((1, length))],
        out_specs=[
            pl.BlockSpec((2, BLK, length), lambda p: (p, 0, 0)),
            col(BLK),
            pl.BlockSpec((1, 8, BLK), lambda p: (p, 0, 0)),
        ],
        out_shape=[
            jax.ShapeDtypeStruct((2 * pairs, BLK, length), bf16),
            jax.ShapeDtypeStruct((BLK, width), f32),
            jax.ShapeDtypeStruct((pairs, 8, BLK), f32),
        ],
        scratch_shapes=[pltpu.VMEM((2, BLK, length), f32)],
        compiler_params=params(),
        name="attend",
    )(q, k, v, near, far, seg_q, seg_k)


def other_probs(k, q, near, far, seg_k, seg_q, lse, scale):
    length, width = q.shape
    pairs = width // PAIR
    wide = length + BLK
    return pl.pallas_call(
        functools.partial(other_probs_kernel, scale, length),
        grid=(pairs,),
        in_specs=[col(BLK), col(length), col(wide), col(wide), full((BLK, 1)), full((1, length)),
                  pl.BlockSpec((1, 8, length), lambda p: (p, 0, 0))],
        out_specs=pl.BlockSpec((2, BLK, length), lambda p: (p, 0, 0)),
        out_shape=jax.ShapeDtypeStruct((2 * pairs, BLK, length), bf16),
        scratch_shapes=[pltpu.VMEM((2, BLK, length), f32)],
        compiler_params=params(),
        name="key_probs",
    )(k, q, near, far, seg_k, seg_q, lse)


def grad_scratch(length):
    return [pltpu.VMEM((2, BLK, length), bf16), pltpu.VMEM((2 * BLK, length + BLK), bf16),
            pltpu.VMEM((2 * BLK, length), bf16)]


def query_grads(p, dctx, ctx, v, q, k, near, scale):
    length, width = k.shape
    pairs = width // PAIR
    wide = length + BLK
    return pl.pallas_call(
        functools.partial(query_grad_kernel, scale, length),
        grid=(pairs,),
        in_specs=[pl.BlockSpec((2, BLK, length), lambda p: (p, 0, 0)), col(BLK), col(BLK), col(length),
                  col(BLK), col(length), col(wide)],
        out_specs=[col(BLK), pl.BlockSpec((PAIR, wide), lambda p: (p, 0))],
        out_shape=[jax.ShapeDtypeStruct((BLK, width), bf16), jax.ShapeDtypeStruct((width, wide), bf16)],
        scratch_shapes=grad_scratch(length),
        compiler_params=params(),
        name="query_grads",
    )(p, dctx, ctx, v, q, k, near)


def key_grads(p, v, dctx, rdot, k, q, near, scale):
    length, width = q.shape
    pairs = width // PAIR
    wide = length + BLK
    return pl.pallas_call(
        functools.partial(key_grad_kernel, scale, length),
        grid=(pairs,),
        in_specs=[pl.BlockSpec((2, BLK, length), lambda p: (p, 0, 0)), col(BLK), col(length),
                  pl.BlockSpec((1, 8, length), lambda p: (p, 0, 0)), col(BLK), col(length), col(wide)],
        out_specs=[col(BLK), col(BLK), pl.BlockSpec((PAIR, wide), lambda p: (p, 0))],
        out_shape=[jax.ShapeDtypeStruct((BLK, width), bf16), jax.ShapeDtypeStruct((BLK, width), bf16),
                   jax.ShapeDtypeStruct((width, wide), bf16)],
        scratch_shapes=grad_scratch(length),
        compiler_params=params(),
        name="key_grads",
    )(p, v, dctx, rdot, k, q, near)


HEADS = 12
EPSILON = 1e-07


def norm_forward(value, gain, shift):
    center = value - jnp.mean(value, axis=-1, keepdims=True)
    scaled = lax.rsqrt(jnp.mean(center * center, axis=-1, keepdims=True) + EPSILON)
    normed = center * scaled
    return (normed * gain + shift, normed, scaled)


def norm_backward(grad_out, normed, scaled, gain):
    grad_normed = grad_out * gain
    inner = grad_normed - jnp.mean(grad_normed, axis=-1, keepdims=True)
    inner = inner - normed * jnp.mean(grad_normed * normed, axis=-1, keepdims=True)
    return (scaled * inner, jnp.sum(grad_out * normed, axis=0), jnp.sum(grad_out, axis=0))


def gelu_exact(value):
    return jax.nn.gelu(value, approximate=False)


def relative_tables(flipped, length, first):
    span = flipped.shape[0] // 2
    side = length - span
    shape = (side, flipped.shape[1])
    padded = jnp.concatenate(
        [jnp.broadcast_to(flipped[:1], shape), flipped, jnp.broadcast_to(flipped[-1:], shape)], axis=0
    )
    near = lax.dynamic_slice_in_dim(padded, length - BLK - first, length + BLK, 0)
    far = lax.dynamic_slice_in_dim(padded, first, length + BLK, 0)
    return near, far


def on_device(
    hidden, segments, rel_embed, query_weight, key_weight, value_weight, output_weight, up_weight, down_weight,
    norm1_gain, norm1_bias, norm2_gain, norm2_bias, cotangent,
):
    tokens, width = hidden.shape[1:]
    span = rel_embed.shape[0] // 2
    scale = 1.0 / math.sqrt(3.0 * (width // HEADS))
    inputs = hidden[0]
    length = lax.axis_size("seq") * tokens
    first = lax.axis_index("seq") * tokens

    def mul(a, b, form=NN):
        return lax.dot_general(a, b, form, preferred_element_type=f32)

    def gather(a, axis):
        return lax.all_gather(a, "seq", axis=axis, tiled=True)

    row_in = gather(inputs, 0)
    row_segs = gather(segments, 1)
    own_segs = segments.reshape(tokens, 1)
    q_all = mul(row_in, query_weight).astype(bf16)
    k_all = mul(row_in, key_weight).astype(bf16)
    v_all = mul(row_in, value_weight).astype(bf16)
    q = mul(inputs, query_weight).astype(bf16)
    k = mul(inputs, key_weight).astype(bf16)
    v = mul(inputs, value_weight).astype(bf16)
    rel_flip = jnp.flip(rel_embed, axis=0)
    qr_near, qr_far = relative_tables(mul(rel_flip, query_weight).astype(bf16), length, first)
    kr_near, kr_far = relative_tables(mul(rel_flip, key_weight).astype(bf16), length, first)

    probs, ctx, lse = forward_attention(q, k_all, v_all, kr_near, qr_far, own_segs, row_segs, scale)
    lse_all = gather(lse, 2)
    probs_t = other_probs(k, q_all, qr_near, kr_far, own_segs, row_segs, lse_all, scale)

    ctx_low = ctx.astype(bf16)
    h1 = inputs.astype(f32) + mul(ctx_low, output_weight)
    normed1, unit1, scaled1 = norm_forward(h1, norm1_gain, norm1_bias)
    normed1_low = normed1.astype(bf16)
    inner = mul(normed1_low, up_weight)
    active, gelu_back = jax.vjp(gelu_exact, inner)
    active_low = active.astype(bf16)
    result, unit2, scaled2 = norm_forward(normed1 + mul(active_low, down_weight), norm2_gain, norm2_bias)
    output = result.astype(bf16)[None]
    cot = cotangent[0].astype(f32)
    d_h2, g_gain2, g_bias2 = norm_backward(cot, unit2, scaled2, norm2_gain)
    d_branch = d_h2.astype(bf16)
    g_down = mul(active_low, d_branch, TN)
    d_inner = gelu_back(mul(d_branch, down_weight, NT))[0].astype(bf16)
    g_up = mul(normed1_low, d_inner, TN)
    d_normed1 = d_h2 + mul(d_inner, up_weight, NT)
    d_h1, g_gain1, g_bias1 = norm_backward(d_normed1, unit1, scaled1, norm1_gain)
    d_attn = d_h1.astype(bf16)
    g_output = mul(ctx_low, d_attn, TN)
    d_ctx = mul(d_attn, output_weight, NT).astype(bf16)

    row_dot = jnp.sum((d_ctx.astype(f32) * ctx).reshape(tokens, HEADS, width // HEADS), axis=2)
    row_dot = jnp.pad(row_dot.T.reshape(HEADS // 2, 2, tokens), ((0, 0), (0, 6), (0, 0)))
    rdot_all = gather(row_dot, 2)
    dctx_all = gather(d_ctx, 0)
    dq, d_kr = query_grads(probs, d_ctx, ctx, v_all, q, k_all, kr_near, scale)
    dk, dv, d_qr = key_grads(probs_t, v, dctx_all, rdot_all, k, q_all, qr_near, scale)

    places = lax.broadcasted_iota(jnp.int32, (length + BLK, 2 * span), 0)
    spots = lax.broadcasted_iota(jnp.int32, (length + BLK, 2 * span), 1)
    select = (jnp.clip(places - first + BLK, 0, 2 * span - 1) == spots).astype(bf16)
    d_qr = mul(d_qr, select).astype(bf16)
    d_kr = mul(d_kr, select).astype(bf16)
    g_query = mul(inputs, dq, TN) + mul(rel_flip, d_qr, (((0,), (1,)), ((), ())))
    g_key = mul(inputs, dk, TN) + mul(rel_flip, d_kr, (((0,), (1,)), ((), ())))
    g_value = mul(inputs, dv, TN)
    both = (((0,), (1,)), ((), ()))
    g_rel = mul(d_qr, query_weight, both) + mul(d_kr, key_weight, both)
    g_rel = jnp.flip(lax.psum(g_rel.astype(bf16), ("seq", "row")).astype(f32), axis=0)

    grad_in = d_h1 + mul(dq, query_weight, NT) + mul(dk, key_weight, NT) + mul(dv, value_weight, NT)

    grads = [g_query, g_key, g_value, g_output, g_up, g_down, g_gain1, g_bias1, g_gain2, g_bias2]
    shares = []
    for g in grads:
        part = lax.psum_scatter(g.astype(bf16), "row", scatter_dimension=0, tiled=True)
        shares.append(lax.psum(part, "seq").astype(f32))
    return (output, grad_in.astype(bf16)[None], *shares, g_rel)


def solution(mesh):
    split = P("row", "seq", None)
    return jax.shard_map(
        on_device,
        mesh=mesh,
        in_specs=(split, P("row", "seq")) + (P(),) * 11 + (split,),
        out_specs=(split, split) + (P("row", None),) * 6 + (P("row"),) * 4 + (P(),),
        check_vma=False,
    )
```

```python
import functools, math
import jax, jax.numpy as jnp
from jax import lax
from jax.experimental import pallas as pl
from jax.experimental.pallas import tpu as pltpu
from jax.sharding import PartitionSpec as P

BLK = 128
PAIR = 128
NT = (((1,), (1,)), ((), ()))
NN = (((1,), (0,)), ((), ()))
TN = (((0,), (0,)), ((), ()))
bf16 = jnp.bfloat16
f32 = jnp.float32


def dot(a, b, form):
    return lax.dot_general(a, b, form, preferred_element_type=f32)


def half_masks(x):
    lane = lax.broadcasted_iota(jnp.int32, x.shape, 1)
    low = lane < PAIR // 2
    zero = jnp.zeros_like(x)
    return jnp.where(low, x, zero), jnp.where(low, zero, x)


def join_heads(stacked, rows):
    lane = lax.broadcasted_iota(jnp.int32, (rows, PAIR), 1)
    return jnp.where(lane < PAIR // 2, stacked[:rows], stacked[rows:])


def slot_order(count):
    return list(range(0, count, 2)) + list(range(1, count, 2))


def block_start(me, slot):
    return pl.multiple_of((me ^ slot) * BLK, BLK)


def fill_scores(me, own_ref, all_ref, near_ref, far_ref, s_ref, n_ref, length):
    wide = length + BLK
    own = jnp.concatenate(half_masks(own_ref[...]), axis=0)
    ext = dot(own, near_ref[...], NT)
    for h in range(2):
        moved = pltpu.roll(ext[h * BLK:(h + 1) * BLK], wide - (BLK - 1), 1, stride=1, stride_axis=0)
        n_ref[h] = moved[:, :length]
    for c, slot in enumerate(slot_order(length // BLK)):
        cols = slice(c * BLK, (c + 1) * BLK)
        blk = all_ref[cols, :]
        both = jnp.concatenate(half_masks(blk), axis=0)
        start = block_start(me, slot)
        win = far_ref[pl.ds(pl.multiple_of(length - BLK - start, BLK), 2 * BLK), :]
        back = dot(both, win, NT)
        direct = dot(own, blk, NT)
        for h in range(2):
            rows = slice(h * BLK, (h + 1) * BLK)
            moved = pltpu.roll(back[rows], BLK + 1, 1, stride=1, stride_axis=0)[:, :BLK]
            s_ref[h, :, cols] = direct[rows] + moved.T + n_ref[h, :, pl.ds(start, BLK)]


def by_slot(me, row):
    length = row.shape[1]
    return jnp.concatenate([row[:, pl.ds(block_start(me, k), BLK)] for k in slot_order(length // BLK)], axis=1)


def forward_kernel(scale, length, me_ref, q_ref, k_ref, v_ref, near_ref, far_ref, segq_ref, segk_ref,
                   p_ref, ctx_ref, lse_ref, s_ref, n_ref):
    me = me_ref[0]
    fill_scores(me, q_ref, k_ref, near_ref, far_ref, s_ref, n_ref, length)
    allowed = segq_ref[...] == by_slot(me, segk_ref)
    stats = []
    for h in range(2):
        logits = jnp.where(allowed, s_ref[h] * scale, -1e30)
        best = jnp.max(logits, axis=1, keepdims=True)
        weights = jnp.exp(logits - best)
        total = jnp.sum(weights, axis=1, keepdims=True)
        p_ref[h] = (weights * (1.0 / total)).astype(bf16)
        stats.append(best + jnp.log(total))
    stacked = jnp.concatenate([p_ref[0], p_ref[1]], axis=0)
    ctx_ref[...] = join_heads(dot(stacked, v_ref[...], NN), BLK)
    lane = lax.broadcasted_iota(jnp.int32, (BLK, BLK), 1)
    tile = jnp.where(lane == 0, stats[0], stats[1])
    lse_ref[0] = tile.T[:8]


def other_probs_kernel(scale, length, me_ref, k_ref, q_ref, near_ref, far_ref, segk_ref, segq_ref, lse_ref, p_ref,
                       s_ref, n_ref):
    me = me_ref[0]
    fill_scores(me, k_ref, q_ref, near_ref, far_ref, s_ref, n_ref, length)
    allowed = segk_ref[...] == by_slot(me, segq_ref)
    for h in range(2):
        logits = s_ref[h] * scale - by_slot(me, lse_ref.at[0, h:h + 1])
        p_ref[h] = jnp.where(allowed, jnp.exp(logits), 0.0).astype(bf16)


def flip_matrix():
    r = lax.broadcasted_iota(jnp.int32, (BLK, BLK), 0)
    c = lax.broadcasted_iota(jnp.int32, (BLK, BLK), 1)
    return jnp.where(r + c == BLK - 1, 1.0, 0.0).astype(bf16)


def fold_table(grad, first, places, fold_ref):
    wide = grad.shape[1]
    place = lax.broadcasted_iota(jnp.int32, grad.shape, 1)
    low = jnp.sum(jnp.where(place < first - BLK, grad, 0.0), axis=1, keepdims=True)
    high = jnp.sum(jnp.where(place >= first + places - BLK, grad, 0.0), axis=1, keepdims=True)
    edge = jnp.zeros((PAIR, BLK), f32)
    fold_ref[:, :BLK] = edge
    fold_ref[:, BLK:BLK + wide] = grad
    fold_ref[:, BLK + wide:] = jnp.zeros((PAIR, places - 3 * BLK), f32)
    table = fold_ref[:, pl.ds(pl.multiple_of(first, BLK), places)]
    spot = lax.broadcasted_iota(jnp.int32, table.shape, 1)
    return table + jnp.where(spot == 0, low, 0.0) + jnp.where(spot == places - 1, high, 0.0)


def grads_tail(scale, length, me, ds_refs, own_ref, all_ref, near_ref, table_ref, wide_ref, down_ref, fold_ref, n_ref):
    flip = flip_matrix()
    for h in range(2):
        back = dot(flip, ds_refs[h], NN)
        down_ref[h * BLK:(h + 1) * BLK, :] = back.astype(bf16)
        for c, slot in enumerate(slot_order(length // BLK)):
            n_ref[:, pl.ds(block_start(me, slot), BLK)] = back[:, c * BLK:(c + 1) * BLK]
        padded = jnp.concatenate([n_ref[...], jnp.zeros((BLK, BLK), f32)], axis=1)
        wide_ref[h * BLK:(h + 1) * BLK, :] = pltpu.roll(padded, 0, 1, stride=1, stride_axis=0).astype(bf16)
    own_grad = dot(down_ref[...], all_ref[...], NN) + dot(wide_ref[...], near_ref[...], NN)
    own_grad = (join_heads(own_grad, BLK) * scale).astype(bf16)
    turned = dot(own_grad, flip, TN).astype(bf16)
    own_grad = dot(flip, own_grad, NN).astype(bf16)
    own = dot(flip, own_ref[...], NN).astype(bf16)
    own = jnp.concatenate(half_masks(own), axis=0)
    near_grad = dot(own, wide_ref[...], TN) * scale
    places = fold_ref.shape[1] - length + BLK
    table_ref[:, :places] = fold_table(near_grad, me * BLK, places, fold_ref).astype(bf16)
    table_ref[:, places:places + BLK] = turned
    return own_grad


def query_grad_kernel(scale, length, me_ref, p_ref, dctx_ref, ctx_ref, v_ref, q_ref, k_ref, near_ref,
                      dq_ref, table_ref, ds_ref, *scratch):
    dctx = jnp.concatenate(half_masks(dctx_ref[...]), axis=0)
    dprob = dot(dctx, v_ref[...], NT)
    ctx = ctx_ref[...]
    for h in range(2):
        rows = slice(h * BLK, (h + 1) * BLK)
        row_dot = jnp.sum(dctx[rows].astype(f32) * ctx, axis=1, keepdims=True)
        ds_ref[h] = (p_ref[h].astype(f32) * (dprob[rows] - row_dot)).astype(bf16)
    dq_ref[...] = grads_tail(scale, length, me_ref[0], ds_ref, q_ref, k_ref, near_ref, table_ref, *scratch)


def key_grad_kernel(scale, length, me_ref, p_ref, v_ref, dctx_ref, rdot_ref, k_ref, q_ref, near_ref,
                    dk_ref, dv_ref, table_ref, ds_ref, *scratch):
    me = me_ref[0]
    vals = jnp.concatenate(half_masks(v_ref[...]), axis=0)
    dctx = dctx_ref[...]
    dprob = dot(vals, dctx, NT)
    for h in range(2):
        rows = slice(h * BLK, (h + 1) * BLK)
        ds_ref[h] = (p_ref[h].astype(f32) * (dprob[rows] - by_slot(me, rdot_ref.at[0, h:h + 1]))).astype(bf16)
    stacked = jnp.concatenate([p_ref[0], p_ref[1]], axis=0)
    dv = join_heads(dot(stacked, dctx, NN), BLK)
    dv_ref[...] = dv.astype(bf16)
    table_ref[:, table_ref.shape[1] - BLK:] = dv.T.astype(bf16)
    dk_ref[...] = grads_tail(scale, length, me, ds_ref, k_ref, q_ref, near_ref, table_ref, *scratch)


def col(rows):
    return pl.BlockSpec((rows, PAIR), lambda p: (0, p))


def full(shape):
    return pl.BlockSpec(shape, lambda p: (0,) * len(shape))


def params():
    return pltpu.CompilerParams(vmem_limit_bytes=56 * 1024 * 1024)


def forward_attention(me, q, k, v, near, far, seg_q, seg_k, scale):
    length, width = k.shape
    pairs = width // PAIR
    wide = length + BLK
    return pl.pallas_call(
        functools.partial(forward_kernel, scale, length),
        grid=(pairs,),
        in_specs=[scalar(), col(BLK), col(length), col(length), col(wide), col(wide), full((BLK, 1)), full((1, length))],
        out_specs=[
            pl.BlockSpec((2, BLK, length), lambda p: (p, 0, 0)),
            col(BLK),
            pl.BlockSpec((1, 8, BLK), lambda p: (p, 0, 0)),
        ],
        out_shape=[
            jax.ShapeDtypeStruct((2 * pairs, BLK, length), bf16),
            jax.ShapeDtypeStruct((BLK, width), f32),
            jax.ShapeDtypeStruct((pairs, 8, BLK), f32),
        ],
        scratch_shapes=[pltpu.VMEM((2, BLK, length), f32), pltpu.VMEM((2, BLK, length), f32)],
        compiler_params=params(),
        name="attend",
    )(me, q, k, v, near, far, seg_q, seg_k)


def other_probs(me, k, q, near, far, seg_k, seg_q, lse, scale):
    length, width = q.shape
    pairs = width // PAIR
    wide = length + BLK
    return pl.pallas_call(
        functools.partial(other_probs_kernel, scale, length),
        grid=(pairs,),
        in_specs=[scalar(), col(BLK), col(length), col(wide), col(wide), full((BLK, 1)), full((1, length)),
                  pl.BlockSpec((1, 8, length), lambda p: (p, 0, 0))],
        out_specs=pl.BlockSpec((2, BLK, length), lambda p: (p, 0, 0)),
        out_shape=jax.ShapeDtypeStruct((2 * pairs, BLK, length), bf16),
        scratch_shapes=[pltpu.VMEM((2, BLK, length), f32), pltpu.VMEM((2, BLK, length), f32)],
        compiler_params=params(),
        name="key_probs",
    )(me, k, q, near, far, seg_k, seg_q, lse)


def grad_scratch(length, places):
    return [
        pltpu.VMEM((2, BLK, length), bf16),
        pltpu.VMEM((2 * BLK, length + BLK), bf16),
        pltpu.VMEM((2 * BLK, length), bf16),
        pltpu.VMEM((PAIR, length + places - BLK), f32),
        pltpu.VMEM((BLK, length), f32),
    ]


def scalar():
    return pl.BlockSpec(memory_space=pltpu.SMEM)


def query_grads(me, p, dctx, ctx, v, q, k, near, places, scale):
    length, width = k.shape
    pairs = width // PAIR
    wide = length + BLK
    return pl.pallas_call(
        functools.partial(query_grad_kernel, scale, length),
        grid=(pairs,),
        in_specs=[scalar(), pl.BlockSpec((2, BLK, length), lambda p: (p, 0, 0)), col(BLK), col(BLK), col(length),
                  col(BLK), col(length), col(wide)],
        out_specs=[col(BLK), pl.BlockSpec((PAIR, places + BLK), lambda p: (p, 0))],
        out_shape=[jax.ShapeDtypeStruct((BLK, width), bf16), jax.ShapeDtypeStruct((width, places + BLK), bf16)],
        scratch_shapes=grad_scratch(length, places),
        compiler_params=params(),
        name="query_grads",
    )(me, p, dctx, ctx, v, q, k, near)


def key_grads(me, p, v, dctx, rdot, k, q, near, places, scale):
    length, width = q.shape
    pairs = width // PAIR
    wide = length + BLK
    return pl.pallas_call(
        functools.partial(key_grad_kernel, scale, length),
        grid=(pairs,),
        in_specs=[scalar(), pl.BlockSpec((2, BLK, length), lambda p: (p, 0, 0)), col(BLK), col(length),
                  pl.BlockSpec((1, 8, length), lambda p: (p, 0, 0)), col(BLK), col(length), col(wide)],
        out_specs=[col(BLK), col(BLK), pl.BlockSpec((PAIR, places + 2 * BLK), lambda p: (p, 0))],
        out_shape=[jax.ShapeDtypeStruct((BLK, width), bf16), jax.ShapeDtypeStruct((BLK, width), bf16),
                   jax.ShapeDtypeStruct((width, places + 2 * BLK), bf16)],
        scratch_shapes=grad_scratch(length, places),
        compiler_params=params(),
        name="key_grads",
    )(me, p, v, dctx, rdot, k, q, near)


def project_kernel(even_ref, odd_ref, wq_ref, wk_ref, wv_ref, q_ref, k_ref, v_ref):
    half = even_ref.shape[0]
    weights = jnp.concatenate([wq_ref[...], wk_ref[...], wv_ref[...]], axis=1)
    for i, ref in enumerate((even_ref, odd_ref)):
        out = dot(ref[...], weights, NN).astype(bf16)
        rows = slice(i * half, (i + 1) * half)
        q_ref[rows] = out[:, :PAIR]
        k_ref[rows] = out[:, PAIR:2 * PAIR]
        v_ref[rows] = out[:, 2 * PAIR:]


def project_rows(even, odd, wq, wk, wv):
    half, width = even.shape
    shape = jax.ShapeDtypeStruct((2 * half, width), bf16)
    return pl.pallas_call(
        project_kernel,
        grid=(width // PAIR,),
        in_specs=[full((half, width)), full((half, width))] + [col(width)] * 3,
        out_specs=[col(2 * half)] * 3,
        out_shape=[shape] * 3,
        compiler_params=params(),
        name="project",
    )(even, odd, wq, wk, wv)


def pack_kernel(cols, rows, me_ref, act_ref, din_ref, ctx_ref, out_ref, turn_ref):
    me = me_ref[0]
    units, width = act_ref.shape[1], ctx_ref.shape[1]

    def turn(ref, count):
        for i in range(count // BLK):
            turn_ref[i * BLK:(i + 1) * BLK, :] = ref[:, i * BLK:(i + 1) * BLK].astype(f32).T

    def pick(count, c):
        size = count // (rows * cols)
        starts = [r * (count // rows) + c * size for r in range(rows)]
        return jnp.concatenate([turn_ref[a:a + size, :] for a in starts], axis=0).astype(bf16)

    chunk = units // cols
    turn(act_ref, units)
    for c in range(cols):
        out_ref[me ^ c, :chunk] = pick(units, c)
    turn(din_ref, units)
    for c in range(cols):
        out_ref[me ^ c, chunk:2 * chunk] = turn_ref[c * chunk:(c + 1) * chunk, :].astype(bf16)
    turn(ctx_ref, width)
    for c in range(cols):
        out_ref[me ^ c, 2 * chunk:] = pick(width, c)


def pack(me, act, din, ctx, cols, rows):
    tokens, units = act.shape
    width = ctx.shape[1]
    return pl.pallas_call(
        functools.partial(pack_kernel, cols, rows),
        in_specs=[scalar()] + [pl.BlockSpec(memory_space=pltpu.VMEM)] * 3,
        out_specs=pl.BlockSpec(memory_space=pltpu.VMEM),
        out_shape=jax.ShapeDtypeStruct((cols, (2 * units + width) // cols, tokens), bf16),
        scratch_shapes=[pltpu.VMEM((units, tokens), f32)],
        compiler_params=params(),
        name="pack",
    )(me, act, din, ctx)


def lanes(parts):
    return jnp.concatenate(parts, axis=1)


def layer_sums_kernel(rows, chunk, me_ref, even_ref, odd_ref, attn_even_ref, attn_odd_ref, *refs):
    *part_refs, out_ref = refs
    me = me_ref[0]
    width = attn_even_ref.shape[2]
    features = part_refs[0].shape[0] - 2 * chunk
    half = width // 2
    down = up = out = 0.0
    for i in range(len(part_refs) // 2):
        part = lanes([part_refs[2 * i][...], part_refs[2 * i + 1][...]])
        normed = jnp.concatenate([even_ref[i, :, :width], odd_ref[i, :, :width]], axis=0)
        branch = jnp.concatenate([even_ref[i, :, width:], odd_ref[i, :, width:]], axis=0)
        attn = jnp.concatenate([attn_even_ref[i], attn_odd_ref[i]], axis=0)
        down = down + dot(part[:chunk], branch, NN)
        up = up + dot(part[chunk:2 * chunk], normed, NN)
        out = out + dot(part[2 * chunk:], attn, NN)
    up = up.T
    share, size, few = width // rows, chunk // rows, features // rows
    for r in range(rows):
        pieces = [
            down[r * size:(r + 1) * size, :half], down[r * size:(r + 1) * size, half:],
            up[r * share:(r + 1) * share],
            out[r * few:(r + 1) * few, :half], out[r * few:(r + 1) * few, half:],
        ]
        out_ref[me ^ r] = jnp.concatenate(pieces, axis=0).astype(bf16)


def layer_sums(row, even, odd, attn_even, attn_odd, parts, rows, chunk):
    width = attn_even.shape[2]
    features = parts[0].shape[0] - 2 * chunk
    height = (2 * chunk + 2 * features) // rows + width // rows
    return pl.pallas_call(
        functools.partial(layer_sums_kernel, rows, chunk),
        in_specs=[scalar()] + [pl.BlockSpec(memory_space=pltpu.VMEM)] * (4 + len(parts)),
        out_specs=pl.BlockSpec(memory_space=pltpu.VMEM),
        out_shape=jax.ShapeDtypeStruct((rows, height, chunk), bf16),
        compiler_params=params(),
        name="layer_sums",
    )(row, even, odd, attn_even, attn_odd, *parts)


def layer_unpack_kernel(cols, me_ref, even_ref, odd_ref, down_ref, up_ref, out_ref):
    me = me_ref[0]
    half = down_ref.shape[1] // 2
    size, share, few = down_ref.shape[0] // cols, up_ref.shape[0], out_ref.shape[0] // cols
    chunk = up_ref.shape[1] // cols
    for ref, odd in ((even_ref, 0), (odd_ref, 1)):
        for i in range(cols // 2):
            spot = me ^ (2 * i + odd)
            part = ref[i].astype(f32)
            down_rows = pl.ds(pl.multiple_of(spot * size, 8), size)
            down_ref[down_rows, :half] = part[:size]
            down_ref[down_rows, half:] = part[size:2 * size]
            at = 2 * size + share
            up_ref[:, pl.ds(pl.multiple_of(spot * chunk, BLK), chunk)] = part[2 * size:at]
            out_rows = pl.ds(pl.multiple_of(spot * few, 8), few)
            out_ref[out_rows, :half] = part[at:at + few]
            out_ref[out_rows, half:] = part[at + few:]


def layer_unpack(me, even, odd, rows, width, units):
    cols = 2 * even.shape[0]
    shapes = [(units // rows, width), (width // rows, units), (width // rows, width)]
    return pl.pallas_call(
        functools.partial(layer_unpack_kernel, cols),
        in_specs=[scalar()] + [pl.BlockSpec(memory_space=pltpu.VMEM)] * 2,
        out_specs=[pl.BlockSpec(memory_space=pltpu.VMEM)] * 3,
        out_shape=[jax.ShapeDtypeStruct(x, f32) for x in shapes],
        compiler_params=params(),
        name="layer_unpack",
    )(me, even, odd)


def attn_sums_kernel(rows, row_ref, even_ref, odd_ref, rel_ref, *refs):
    *refs, out_ref = refs
    count = len(refs) // 2
    me = row_ref[0]
    size = refs[0].shape[0]
    width, places = even_ref.shape[2], rel_ref.shape[0]
    table = {"q": 0.0, "k": 0.0}
    total = {"q": 0.0, "k": 0.0, "v": 0.0}
    for i in range(count // 2):
        rows_in = jnp.concatenate([even_ref[i], odd_ref[i]], axis=0)
        qa, qb, ka, kb = refs[2 * i], refs[2 * i + 1], refs[count + 2 * i], refs[count + 2 * i + 1]
        cut = lambda ref, j: ref[:, places + j * BLK:places + (j + 1) * BLK]
        total["q"] = total["q"] + dot(lanes([cut(qa, 0), cut(qb, 0)]), rows_in, NN)
        total["k"] = total["k"] + dot(lanes([cut(ka, 0), cut(kb, 0)]), rows_in, NN)
        total["v"] = total["v"] + dot(lanes([cut(ka, 1), cut(kb, 1)]), rows_in, NN)
        table["k"] = table["k"] + qa[:, :places].astype(f32) + qb[:, :places].astype(f32)
        table["q"] = table["q"] + ka[:, :places].astype(f32) + kb[:, :places].astype(f32)
    pieces = []
    for name in ("q", "k"):
        pieces.append(total[name] + dot(table[name].astype(bf16), rel_ref[...], NN))
    pieces.append(total["v"])
    fill = -3 * size % BLK
    if fill:
        pieces.append(jnp.zeros((fill, width), f32))
    full_sum = jnp.concatenate(pieces, axis=0).T
    share, spots = width // rows, places // rows
    wide = full_sum.shape[1]
    both = jnp.concatenate([table["q"], table["k"]], axis=0)
    lines = 2 * size * spots // wide
    for r in range(rows):
        cut = both[:, r * spots:(r + 1) * spots]
        cut = lanes([cut[j * lines:(j + 1) * lines] for j in range(wide // spots)])
        out_ref[me ^ r] = jnp.concatenate([full_sum[r * share:(r + 1) * share], cut], axis=0).astype(bf16)


def attn_sums(row, even, odd, rel, q_parts, k_parts, rows):
    size = q_parts[0].shape[0]
    width, places = even.shape[2], rel.shape[0]
    wide = 3 * size + (-3 * size % BLK)
    height = width // rows + 2 * size * (places // rows) // wide
    return pl.pallas_call(
        functools.partial(attn_sums_kernel, rows),
        in_specs=[scalar()] + [pl.BlockSpec(memory_space=pltpu.VMEM)] * (3 + len(q_parts) + len(k_parts)),
        out_specs=pl.BlockSpec(memory_space=pltpu.VMEM),
        out_shape=jax.ShapeDtypeStruct((rows, height, wide), bf16),
        compiler_params=params(),
        name="attn_sums",
    )(row, even, odd, rel, *q_parts, *k_parts)


def attn_unpack_kernel(cols, spots, me_ref, even_ref, odd_ref, wq_ref, wk_ref, q_ref, k_ref, v_ref, rel_ref, all_ref, tq_ref, tk_ref):
    me = me_ref[0]
    share, width = q_ref.shape
    size = width // cols
    for ref, odd in ((even_ref, 0), (odd_ref, 1)):
        for i in range(cols // 2):
            all_ref[me ^ (2 * i + odd)] = ref[i].astype(f32)
    wide = all_ref.shape[2]
    lines = all_ref.shape[1] - share
    for c in range(cols):
        spot = slice(c * size, (c + 1) * size)
        q_ref[:, spot] = all_ref[c, :share, :size]
        k_ref[:, spot] = all_ref[c, :share, size:2 * size]
        v_ref[:, spot] = all_ref[c, :share, 2 * size:3 * size]
        tail = all_ref[c, share:, :]
        tail = jnp.concatenate([tail[:, j * spots:(j + 1) * spots] for j in range(wide // spots)], axis=0)
        tq_ref[spot, :] = tail[:size].astype(bf16)
        tk_ref[spot, :] = tail[size:].astype(bf16)
    flip = flip_matrix()
    turned_q = dot(tq_ref[...], flip, NN).astype(bf16)
    turned_k = dot(tk_ref[...], flip, NN).astype(bf16)
    across = (((0,), (1,)), ((), ()))
    rel_ref[...] = (dot(turned_q, wq_ref[...], across) + dot(turned_k, wk_ref[...], across)).astype(bf16)


def attn_unpack(me, even, odd, wq, wk, rows, places):
    cols = 2 * even.shape[0]
    width = wq.shape[0]
    share, spots = width // rows, places // rows
    shape = jax.ShapeDtypeStruct((share, width), f32)
    return pl.pallas_call(
        functools.partial(attn_unpack_kernel, cols, spots),
        in_specs=[scalar()] + [pl.BlockSpec(memory_space=pltpu.VMEM)] * 4,
        out_specs=[pl.BlockSpec(memory_space=pltpu.VMEM)] * 4,
        out_shape=[shape] * 3 + [jax.ShapeDtypeStruct((spots, width), bf16)],
        scratch_shapes=[pltpu.VMEM((cols,) + even.shape[1:], f32), pltpu.VMEM((width, spots), bf16),
                        pltpu.VMEM((width, spots), bf16)],
        compiler_params=params(),
        name="attn_unpack",
    )(me, even, odd, wq, wk)


HEADS = 12
EPSILON = 1e-07


def norm_forward(value, gain, shift):
    center = value - jnp.mean(value, axis=-1, keepdims=True)
    scaled = lax.rsqrt(jnp.mean(center * center, axis=-1, keepdims=True) + EPSILON)
    normed = center * scaled
    return (normed * gain + shift, normed, scaled)


def norm_backward(grad_out, normed, scaled, gain):
    grad_normed = grad_out * gain
    inner = grad_normed - jnp.mean(grad_normed, axis=-1, keepdims=True)
    inner = inner - normed * jnp.mean(grad_normed * normed, axis=-1, keepdims=True)
    return (scaled * inner, jnp.sum(grad_out * normed, axis=0), jnp.sum(grad_out, axis=0))


def gelu_exact(value):
    return jax.nn.gelu(value, approximate=False)


def mul(a, b, form=NN):
    return lax.dot_general(a, b, form, preferred_element_type=f32)


def swap(x, axis, k):
    return lax.ppermute(x, axis, [(i, i ^ k) for i in range(lax.axis_size(axis))])


def gather(x):
    even = jnp.stack([x] + [swap(x, "seq", k) for k in range(2, lax.axis_size("seq"), 2)])
    return even, swap(even, "seq", 1)


def gather_small(x, axis):
    count = lax.axis_size(axis)
    out = jnp.zeros((count,) + x.shape, x.dtype)
    out = lax.dynamic_update_slice_in_dim(out, x[None], lax.axis_index(axis), 0)
    k = 1
    while k < count:
        out = out + swap(out, axis, k)
        k *= 2
    return out


def deal(x, axis):
    return [x[0]] + [swap(x[k], axis, k) for k in range(1, lax.axis_size(axis))]


def sum_small(x):
    for axis in ("seq", "row"):
        k = 1
        while k < lax.axis_size(axis):
            x = x + swap(x, axis, k)
            k *= 2
    return x


def relative_tables(flipped, length, first):
    span = flipped.shape[0] // 2
    side = length - span
    shape = (side, flipped.shape[1])
    padded = jnp.concatenate(
        [jnp.broadcast_to(flipped[:1], shape), flipped, jnp.broadcast_to(flipped[-1:], shape)], axis=0
    )
    near = lax.dynamic_slice_in_dim(padded, length - BLK - first, length + BLK, 0)
    far = lax.dynamic_slice_in_dim(padded, first, length + BLK, 0)
    return near, far


def flip_rows(count):
    r = lax.broadcasted_iota(jnp.int32, (count, count), 0)
    c = lax.broadcasted_iota(jnp.int32, (count, count), 1)
    return (r + c == count - 1).astype(bf16)


def reduced(g):
    part = lax.psum_scatter(g.astype(bf16), "row", scatter_dimension=0, tiled=True)
    return lax.psum(part, "seq").astype(f32)


def on_device(
    hidden, segments, rel_embed, query_weight, key_weight, value_weight, output_weight, up_weight, down_weight,
    norm1_gain, norm1_bias, norm2_gain, norm2_bias, cotangent,
):
    tokens, width = hidden.shape[1:]
    places = rel_embed.shape[0]
    units = up_weight.shape[1]
    heads = HEADS
    pairs = width // PAIR
    scale = 1.0 / math.sqrt(3.0 * (width // heads))
    inputs = hidden[0]
    cols, rows = lax.axis_size("seq"), lax.axis_size("row")
    length = cols * tokens
    place = lax.axis_index("seq")
    first = place * tokens
    me = place.reshape(1).astype(jnp.int32)
    row = lax.axis_index("row").reshape(1).astype(jnp.int32)
    share = width // rows
    dealt = (units // (rows * cols)) % 16 == 0 and places // rows == BLK

    in_even, in_odd = gather(inputs)
    row_segs = gather_small(segments, "seq").reshape(1, length)
    own_segs = segments.reshape(tokens, 1)
    rel_flip = mul(flip_rows(places), rel_embed).astype(bf16)
    qr_near, qr_far = relative_tables(mul(rel_flip, query_weight).astype(bf16), length, first)
    kr_near, kr_far = relative_tables(mul(rel_flip, key_weight).astype(bf16), length, first)
    half = (length // 2, width)
    q, k, v = project_rows(in_even.reshape(half), in_odd.reshape(half), query_weight, key_weight, value_weight)

    probs, ctx, lse = forward_attention(me, q, k, v, kr_near, qr_far, own_segs, row_segs, scale)

    ctx_low = ctx.astype(bf16)
    h1 = inputs.astype(f32) + mul(ctx_low, output_weight)
    normed1, unit1, scaled1 = norm_forward(h1, norm1_gain, norm1_bias)
    normed1_low = normed1.astype(bf16)
    inner = mul(normed1_low, up_weight)
    active, gelu_back = jax.vjp(gelu_exact, inner)
    active_low = active.astype(bf16)
    result, unit2, scaled2 = norm_forward(normed1 + mul(active_low, down_weight), norm2_gain, norm2_bias)
    output = result.astype(bf16)[None]
    cot = cotangent[0].astype(f32)
    d_h2, g_gain2, g_bias2 = norm_backward(cot, unit2, scaled2, norm2_gain)
    d_branch = d_h2.astype(bf16)
    d_inner = gelu_back(mul(d_branch, down_weight, NT))[0].astype(bf16)
    d_normed1 = d_h2 + mul(d_inner, up_weight, NT)
    d_h1, g_gain1, g_bias1 = norm_backward(d_normed1, unit1, scaled1, norm1_gain)
    d_attn = d_h1.astype(bf16)
    d_ctx = mul(d_attn, output_weight, NT).astype(bf16)
    row_dot = jnp.sum((d_ctx.astype(f32) * ctx).reshape(tokens, heads, width // heads), axis=2)

    stats = jnp.concatenate([lse[:, :2].reshape(heads, tokens), row_dot.T], axis=0)
    stats = gather_small(stats, "seq").reshape(cols, 2, pairs, 2, tokens).transpose(1, 2, 3, 0, 4)
    lse_all, rdot_all = jnp.pad(stats.reshape(2, pairs, 2, length), ((0, 0), (0, 0), (0, 6), (0, 0)))
    probs_t = other_probs(me, k, q, qr_near, kr_far, own_segs, row_segs, lse_all, scale)
    attn_even, attn_odd = gather(d_attn)
    dctx_all = jnp.concatenate([attn_even.reshape(half), attn_odd.reshape(half)], axis=0)
    dctx_all = mul(dctx_all, output_weight, NT).astype(bf16)
    dq, q_table = query_grads(me, probs, d_ctx, ctx, v, q, k, kr_near, places, scale)
    dk, dv, k_table = key_grads(me, probs_t, v, dctx_all, rdot_all, k, q, qr_near, places, scale)
    grad_in = d_h1 + mul(dq, query_weight, NT) + mul(dk, key_weight, NT) + mul(dv, value_weight, NT)

    if dealt:
        chunk = units // cols
        branch_even, branch_odd = gather(jnp.concatenate([normed1_low, d_branch], axis=1))
        parts = deal(pack(me, active_low, d_inner, ctx, cols, rows), "seq")
        sums = layer_sums(row, branch_even, branch_odd, attn_even, attn_odd, parts, rows, chunk)
        sums = sum(x.astype(f32) for x in deal(sums, "row")).astype(bf16)
        g_down, g_up, g_output = layer_unpack(me, *gather(sums), rows, width, units)
        q_parts = deal_dynamic(q_table, cols)
        k_parts = deal_dynamic(k_table, cols)
        sums = attn_sums(row, in_even, in_odd, rel_flip, q_parts, k_parts, rows)
        sums = sum(x.astype(f32) for x in deal(sums, "row")).astype(bf16)
        g_query, g_key, g_value, g_rel = attn_unpack(me, *gather(sums), query_weight, key_weight, rows, places)
        blocks = [g_rel] + [swap(g_rel, "row", k) for k in range(1, rows)]
        out = jnp.zeros((rows,) + g_rel.shape, bf16)
        for k, block in enumerate(blocks):
            out = lax.dynamic_update_slice_in_dim(out, block[None], rows - 1 - (row[0] ^ k), 0)
        g_rel = out.reshape(places, width).astype(f32)
    else:
        g_down = reduced(mul(active_low, d_branch, TN))
        g_up = reduced(mul(normed1_low, d_inner, TN))
        g_output = reduced(mul(ctx_low, d_attn, TN))
        across = (((0,), (1,)), ((), ()))
        d_kr, d_qr = q_table[:, :places], k_table[:, :places]
        g_query = reduced(mul(inputs, dq, TN) + mul(rel_flip, d_qr, across))
        g_key = reduced(mul(inputs, dk, TN) + mul(rel_flip, d_kr, across))
        g_value = reduced(mul(inputs, dv, TN))
        g_rel = mul(d_qr, query_weight, across) + mul(d_kr, key_weight, across)
        g_rel = lax.psum(mul(flip_rows(places), g_rel.astype(bf16)).astype(bf16), ("seq", "row")).astype(f32)

    small = sum_small(jnp.stack([g_gain1, g_bias1, g_gain2, g_bias2]))
    small = lax.dynamic_slice_in_dim(small, lax.axis_index("row") * share, share, 1)
    return (
        output, grad_in.astype(bf16)[None], g_query, g_key, g_value, g_output, g_up, g_down,
        small[0], small[1], small[2], small[3], g_rel,
    )


def deal_dynamic(x, cols):
    size = x.shape[0] // cols
    me = lax.axis_index("seq")
    parts = [lax.dynamic_slice_in_dim(x, (me ^ k) * size, size, 0) for k in range(cols)]
    return [parts[0]] + [swap(parts[k], "seq", k) for k in range(1, cols)]


def solution(mesh):
    split = P("row", "seq", None)
    return jax.shard_map(
        on_device,
        mesh=mesh,
        in_specs=(split, P("row", "seq")) + (P(),) * 11 + (split,),
        out_specs=(split, split) + (P("row", None),) * 6 + (P("row"),) * 4 + (P(),),
        check_vma=False,
    )
```

```python
import functools, math
import jax, jax.numpy as jnp
from jax import lax
from jax.experimental import pallas as pl
from jax.experimental.pallas import tpu as pltpu
from jax.sharding import PartitionSpec as P

BLK = 256
TOK = 128
PAIR = 128
EXTRA = 16
COST = 3e8
NT = (((1,), (1,)), ((), ()))
NN = (((1,), (0,)), ((), ()))
TN = (((0,), (0,)), ((), ()))
bf16 = jnp.bfloat16
f32 = jnp.float32


def dot(a, b, form):
    return lax.dot_general(a, b, form, preferred_element_type=f32)


def lanes(parts):
    return jnp.concatenate(parts, axis=1)


def half_masks(x):
    lane = lax.broadcasted_iota(jnp.int32, x.shape, 1)
    low = lane < PAIR // 2
    zero = jnp.zeros_like(x)
    return jnp.where(low, x, zero), jnp.where(low, zero, x)


def join_heads(stacked, rows):
    lane = lax.broadcasted_iota(jnp.int32, (rows, PAIR), 1)
    return jnp.where(lane < PAIR // 2, stacked[:rows], stacked[rows:])


def block_start(chip, slot):
    return pl.multiple_of((chip ^ slot) * BLK, BLK)


def fill_table(out_ref, flip_ref, start):
    places = flip_ref.shape[0]
    low = jnp.broadcast_to(flip_ref[0:1, :], (BLK, PAIR))
    high = jnp.broadcast_to(flip_ref[places - 1:places, :], (BLK, PAIR))
    for b in range(out_ref.shape[0] // BLK):
        out_ref[b * BLK:(b + 1) * BLK, :] = jnp.where(b * BLK < start, low, high)
    out_ref[pl.ds(pl.multiple_of(start, BLK), places), :] = flip_ref[...]


def fill_scores(chip, own_ref, all_ref, near_ref, far_ref, s_ref, n_ref, length):
    wide = length + BLK
    own = jnp.concatenate(half_masks(own_ref[...]), axis=0)
    ext = dot(own, near_ref[...], NT)
    for h in range(2):
        moved = pltpu.roll(ext[h * BLK:(h + 1) * BLK], wide - (BLK - 1), 1, stride=1, stride_axis=0)
        n_ref[h] = moved[:, :length]
    for slot in range(length // BLK):
        cols = slice(slot * BLK, (slot + 1) * BLK)
        blk = all_ref[cols, :]
        both = jnp.concatenate(half_masks(blk), axis=0)
        start = block_start(chip, slot)
        win = far_ref[pl.ds(pl.multiple_of(length - BLK - start, BLK), 2 * BLK), :]
        back = dot(both, win, NT)
        direct = dot(own, blk, NT)
        for h in range(2):
            rows = slice(h * BLK, (h + 1) * BLK)
            moved = pltpu.roll(back[rows], BLK + 1, 1, stride=1, stride_axis=0)[:, :BLK]
            s_ref[h, :, cols] = direct[rows] + moved.T + n_ref[h, :, pl.ds(start, BLK)]


def far_start(chip, length):
    return length - BLK - chip * BLK


def forward_kernel(scale, length, place_ref, q_ref, k_ref, v_ref, near_ref, far_ref, segq_ref, segk_ref,
                   p_ref, out_ref, s_ref, n_ref, near_tab, far_tab):
    chip = place_ref[0]
    fill_table(near_tab, near_ref, chip * BLK)
    fill_table(far_tab, far_ref, far_start(chip, length))
    fill_scores(chip, q_ref, k_ref, near_tab, far_tab, s_ref, n_ref, length)
    allowed = segq_ref[...] == segk_ref[...]
    stats = []
    for h in range(2):
        logits = jnp.where(allowed, s_ref[h] * scale, -1e30)
        best = jnp.max(logits, axis=1, keepdims=True)
        weights = jnp.exp(logits - best)
        total = jnp.sum(weights, axis=1, keepdims=True)
        p_ref[h] = (weights * (1.0 / total)).astype(bf16)
        stats.append(best + jnp.log(total))
    stacked = jnp.concatenate([p_ref[0], p_ref[1]], axis=0)
    ctx = join_heads(dot(stacked, v_ref[...], NN), BLK)
    lane = lax.broadcasted_iota(jnp.int32, (TOK, PAIR), 1)
    for c in range(2):
        rows = slice(c * TOK, (c + 1) * TOK)
        out_ref[c, :TOK, :] = ctx[rows]
        out_ref[c, TOK:, :] = jnp.where(lane == 0, stats[0][rows], stats[1][rows]).T[:8]


def flip_matrix(count):
    r = lax.broadcasted_iota(jnp.int32, (count, count), 0)
    c = lax.broadcasted_iota(jnp.int32, (count, count), 1)
    return jnp.where(r + c == count - 1, 1.0, 0.0).astype(bf16)


def fold_table(grad, start, places, fold_ref):
    place = lax.broadcasted_iota(jnp.int32, grad.shape, 1)
    low = jnp.sum(jnp.where(place < start, grad, 0.0), axis=1, keepdims=True)
    high = jnp.sum(jnp.where(place >= start + places, grad, 0.0), axis=1, keepdims=True)
    fold_ref[...] = grad
    table = fold_ref[:, pl.ds(pl.multiple_of(start, BLK), places)]
    spot = lax.broadcasted_iota(jnp.int32, table.shape, 1)
    return table + jnp.where(spot == 0, low, 0.0) + jnp.where(spot == places - 1, high, 0.0)


def grads_tail(scale, length, places, chip, ds_ref, own_ref, all_ref, near_ref, table_ref, wide_ref, down_ref, fold_ref, n_ref):
    flip = flip_matrix(BLK)
    rows = pair_rows()
    for h in range(2):
        back = dot(flip, ds_ref[h], NN)
        down_ref[h * BLK:(h + 1) * BLK, :] = back.astype(bf16)
        for slot in range(length // BLK):
            n_ref[h, :, pl.ds(block_start(chip, slot), BLK)] = back[:, slot * BLK:(slot + 1) * BLK]
        padded = lanes([n_ref[h], jnp.zeros((BLK, BLK), f32)])
        wide_ref[h * BLK:(h + 1) * BLK, :] = pltpu.roll(padded, 0, 1, stride=1, stride_axis=0).astype(bf16)
    own_grad = dot(down_ref[...], all_ref[...], NN) + dot(wide_ref[...], near_ref[...], NN)
    own_grad = (join_heads(own_grad, BLK) * scale).astype(bf16)
    table_ref[rows, places:places + BLK] = dot(own_grad, flip, TN).astype(bf16)
    own_grad = dot(flip, own_grad, NN).astype(bf16)
    own = dot(flip, own_ref[...], NN).astype(bf16)
    own = jnp.concatenate(half_masks(own), axis=0)
    near_grad = dot(own, wide_ref[...], TN) * scale
    table_ref[rows, :places] = fold_table(near_grad, chip * BLK, places, fold_ref).astype(bf16)
    return own_grad


def pair_rows():
    return pl.ds(pl.multiple_of(pl.program_id(0) * PAIR, PAIR), PAIR)


def deal_table(chip, table_ref, out_refs):
    @pl.when(pl.program_id(0) == pl.num_programs(0) - 1)
    def _():
        for k, ref in enumerate(out_refs):
            size = ref.shape[0]
            ref[...] = table_ref[pl.ds(pl.multiple_of((chip ^ k) * size, EXTRA), size), :]


def split_tokens(out_ref, value):
    for c in range(2):
        out_ref[c] = value[c * TOK:(c + 1) * TOK]


def query_grad_kernel(scale, length, chips, place_ref, p_ref, mine_ref, twin_ref, out_weight_ref, ctx_ref, v_ref, q_ref, k_ref,
                      near_ref, earlier_ref, dq_ref, *refs):
    out_refs, (near_tab, dctx_ref, table_ref, ds_ref, *scratch) = refs[:chips], refs[chips:]
    chip, core = place_ref[0], place_ref[1]
    places = near_ref.shape[0]
    fill_table(near_tab, near_ref, chip * BLK)
    for ref, at in ((mine_ref, core), (twin_ref, 1 - core)):
        rows = pl.ds(pl.multiple_of(at * TOK, TOK), TOK)
        dctx_ref[rows, :] = dot(ref[:TOK, :], out_weight_ref[...], NT).astype(bf16)
    dctx = jnp.concatenate(half_masks(dctx_ref[...]), axis=0)
    dprob = dot(dctx, v_ref[...], NT)
    ctx = jnp.concatenate([ctx_ref[0, :TOK, :], ctx_ref[1, :TOK, :]], axis=0)
    for h in range(2):
        rows = slice(h * BLK, (h + 1) * BLK)
        row_dot = jnp.sum(dctx[rows].astype(f32) * ctx, axis=1, keepdims=True)
        ds_ref[h] = (p_ref[h].astype(f32) * (dprob[rows] - row_dot)).astype(bf16)
    dq = grads_tail(scale, length, places, chip, ds_ref, q_ref, k_ref, near_tab, table_ref, *scratch)
    split_tokens(dq_ref, dq)
    deal_table(chip, table_ref, out_refs)


def key_grad_kernel(scale, length, pairs, chips, place_ref, k_ref, v_ref, q_ref, near_ref, far_ref, segk_ref, segq_ref,
                    mine_ref, twin_ref, even_ref, odd_ref, out_weight_ref, earlier_ref, dk_ref, dv_ref, *refs):
    out_refs, refs = refs[:chips], refs[chips:]
    s_ref, near_tab, far_tab, dctx_ref, p_ref, stat_ref, table_ref, ds_ref, *scratch = refs
    chip, core = place_ref[0], place_ref[1]
    places = near_ref.shape[0]
    fill_table(near_tab, near_ref, chip * BLK)
    fill_table(far_tab, far_ref, far_start(chip, length))
    fill_scores(chip, k_ref, q_ref, near_tab, far_tab, s_ref, scratch[-1], length)
    stat_cols = pl.ds(pl.multiple_of((core * pairs + pl.program_id(0)) * PAIR, PAIR), PAIR)
    for slot in range(length // BLK):
        for odd in range(2):
            at = pl.ds(pl.multiple_of(slot * BLK + (core ^ odd) * TOK, TOK), TOK)
            if slot == 0:
                ref = twin_ref if odd else mine_ref
            else:
                ref = (odd_ref if odd else even_ref).at[slot - 1]
            dctx_ref[at, :] = dot(ref[:TOK, :], out_weight_ref[...], NT).astype(bf16)
            stat_ref[:, at] = ref[TOK:, stat_cols].astype(f32)
    merged = [stat_ref[3 * j:3 * j + 1] + stat_ref[3 * j + 1:3 * j + 2] + stat_ref[3 * j + 2:3 * j + 3] for j in range(4)]
    allowed = segk_ref[...] == segq_ref[...]
    dctx = dctx_ref[...]
    vals = jnp.concatenate(half_masks(v_ref[...]), axis=0)
    dprob = dot(vals, dctx, NT)
    for h in range(2):
        rows = slice(h * BLK, (h + 1) * BLK)
        probs = jnp.where(allowed, jnp.exp(s_ref[h] * scale - merged[h]), 0.0)
        p_ref[rows, :] = probs.astype(bf16)
        ds_ref[h] = (probs * (dprob[rows] - merged[2 + h])).astype(bf16)
    dv = join_heads(dot(p_ref[...], dctx, NN), BLK)
    split_tokens(dv_ref, dv.astype(bf16))
    table_ref[pair_rows(), places + BLK:] = dv.T.astype(bf16)
    dk = grads_tail(scale, length, places, chip, ds_ref, k_ref, q_ref, near_tab, table_ref, *scratch)
    split_tokens(dk_ref, dk)
    deal_table(chip, table_ref, out_refs)


def col(rows):
    return pl.BlockSpec((rows, PAIR), lambda p: (0, p))


def full(shape):
    return pl.BlockSpec(shape, lambda p: (0,) * len(shape))


def whole():
    return pl.BlockSpec(memory_space=pltpu.VMEM)


def scalar():
    return pl.BlockSpec(memory_space=pltpu.SMEM)


def unread():
    return pl.BlockSpec(memory_space=pl.ANY)


def params():
    return pltpu.CompilerParams(vmem_limit_bytes=56 * 1024 * 1024)


def cost(microseconds):
    return pl.CostEstimate(flops=int(microseconds * COST), bytes_accessed=0, transcendentals=0)


def after(x, *earlier):
    def kernel(*refs):
        pass

    return pl.pallas_call(
        kernel,
        in_specs=[unread()] * (1 + len(earlier)),
        out_specs=unread(),
        out_shape=jax.ShapeDtypeStruct(x.shape, x.dtype),
        input_output_aliases={0: 0},
        cost_estimate=cost(0.1),
        name="after",
    )(x, *earlier)


def stack_kernel(count, *refs):
    for i in range(count):
        refs[-1][i] = refs[i][...]


def stack(arrays, *earlier):
    count = len(arrays)
    return pl.pallas_call(
        functools.partial(stack_kernel, count),
        in_specs=[whole()] * count + [unread()] * len(earlier),
        out_specs=whole(),
        out_shape=jax.ShapeDtypeStruct((count,) + arrays[0].shape, arrays[0].dtype),
        compiler_params=params(),
        cost_estimate=cost(1),
        name="stack",
    )(*arrays, *earlier)


def table_scratch(length):
    return pltpu.VMEM((length + BLK, PAIR), bf16)


def probs_block(length):
    return pl.BlockSpec((2, BLK, length), lambda p: (p, 0, 0))


def token_block():
    return pl.BlockSpec((2, TOK, PAIR), lambda p: (0, 0, p))


def forward_attention(place, q, k, v, near, far, seg_q, seg_k, scale):
    length, width = k.shape
    places = near.shape[0]
    pairs = width // PAIR
    return pl.pallas_call(
        functools.partial(forward_kernel, scale, length),
        grid=(pairs,),
        in_specs=[scalar(), col(BLK), col(length), col(length), col(places), col(places), full((BLK, 1)), full((1, length))],
        out_specs=[probs_block(length), pl.BlockSpec((2, TOK + 8, PAIR), lambda p: (0, 0, p))],
        out_shape=[
            jax.ShapeDtypeStruct((2 * pairs, BLK, length), bf16),
            jax.ShapeDtypeStruct((2, TOK + 8, width), f32),
        ],
        scratch_shapes=[pltpu.VMEM((2, BLK, length), f32)] * 2 + [table_scratch(length)] * 2,
        compiler_params=params(),
        cost_estimate=cost(14),
        name="attend",
    )(place, q, k, v, near, far, seg_q, seg_k)


def grad_scratch(length):
    return [
        pltpu.VMEM((2, BLK, length), bf16),
        pltpu.VMEM((2 * BLK, length + BLK), bf16),
        pltpu.VMEM((2 * BLK, length), bf16),
        pltpu.VMEM((PAIR, length + BLK), f32),
        pltpu.VMEM((2, BLK, length), f32),
    ]


def query_grads(place, p, mine, twin, out_weight, ctx, v, q, k, near, earlier, scale):
    length, width = k.shape
    places = near.shape[0]
    chips = length // BLK
    table = jax.ShapeDtypeStruct((width // chips, places + BLK), bf16)
    return pl.pallas_call(
        functools.partial(query_grad_kernel, scale, length, chips),
        grid=(width // PAIR,),
        in_specs=[scalar(), probs_block(length), full(mine.shape), full(twin.shape),
                  pl.BlockSpec((PAIR, out_weight.shape[1]), lambda p: (p, 0)),
                  pl.BlockSpec((2, TOK + 8, PAIR), lambda p: (0, 0, p)), col(length), col(BLK), col(length), col(places),
                  unread()],
        out_specs=[token_block()] + [full(table.shape)] * chips,
        out_shape=[jax.ShapeDtypeStruct((2, TOK, width), bf16)] + [table] * chips,
        scratch_shapes=[table_scratch(length), pltpu.VMEM((BLK, PAIR), bf16), pltpu.VMEM((width, places + BLK), bf16)]
        + grad_scratch(length),
        compiler_params=params(),
        cost_estimate=cost(1),
        name="query_grads",
    )(place, p, mine, twin, out_weight, ctx, v, q, k, near, earlier)


def key_grads(place, k, v, q, near, far, seg_k, seg_q, attn, out_weight, earlier, scale):
    length, width = q.shape
    places = near.shape[0]
    pairs = width // PAIR
    chips = length // BLK
    table = jax.ShapeDtypeStruct((width // chips, places + 2 * BLK), bf16)
    return pl.pallas_call(
        functools.partial(key_grad_kernel, scale, length, pairs, chips),
        grid=(pairs,),
        in_specs=[scalar(), col(BLK), col(BLK), col(length), col(places), col(places), full((BLK, 1)), full((1, length))]
        + [full(x.shape) for x in attn]
        + [pl.BlockSpec((PAIR, out_weight.shape[1]), lambda p: (p, 0)), unread()],
        out_specs=[token_block(), token_block()] + [full(table.shape)] * chips,
        out_shape=[jax.ShapeDtypeStruct((2, TOK, width), bf16)] * 2 + [table] * chips,
        scratch_shapes=[pltpu.VMEM((2, BLK, length), f32), table_scratch(length), table_scratch(length),
                        pltpu.VMEM((length, PAIR), bf16), pltpu.VMEM((2 * BLK, length), bf16),
                        pltpu.VMEM((EXTRA, length), f32), pltpu.VMEM((width, places + 2 * BLK), bf16)]
        + grad_scratch(length),
        compiler_params=params(),
        cost_estimate=cost(1),
        name="key_grads",
    )(place, k, v, q, near, far, seg_k, seg_q, *attn, out_weight, earlier)


def attn_out_kernel(dattn_ref, weight_ref, ctx_ref, vec_ref, pay_ref):
    tokens, width = dattn_ref.shape
    dattn = dattn_ref[...]
    pay_ref[:tokens, :] = dattn
    half = PAIR // 2
    for p in range(width // PAIR):
        cols = slice(p * PAIR, (p + 1) * PAIR)
        dctx = dot(dattn, weight_ref[cols, :], NT).astype(bf16)
        turned = (dctx.astype(f32) * ctx_ref[:tokens, cols]).T
        rows = [ctx_ref[tokens:tokens + 1, cols], ctx_ref[tokens + 1:tokens + 2, cols],
                jnp.sum(turned[:half], axis=0, keepdims=True), jnp.sum(turned[half:], axis=0, keepdims=True)]
        pieces = []
        for value in rows:
            for _ in range(3):
                piece = value.astype(bf16).astype(f32)
                pieces.append(piece)
                value = value - piece
        pieces.append(vec_ref[:, cols])
        pay_ref[tokens:, cols] = jnp.concatenate(pieces, axis=0).astype(bf16)


def attn_out(dattn, weight, ctx, vectors):
    tokens, width = dattn.shape
    return pl.pallas_call(
        attn_out_kernel,
        in_specs=[whole()] * 4,
        out_specs=whole(),
        out_shape=jax.ShapeDtypeStruct((tokens + EXTRA, width), bf16),
        compiler_params=params(),
        cost_estimate=cost(2),
        name="attn_out",
    )(dattn, weight, ctx, vectors)


def project_kernel(place_ref, mine_ref, twin_ref, even_ref, odd_ref, wq_ref, wk_ref, wv_ref, q_ref, k_ref, v_ref, seg_ref,
                   rows_ref):
    core = place_ref[1]
    count = even_ref.shape[0] + 1

    @pl.when(pl.program_id(0) == 0)
    def _():
        for slot in range(count):
            for odd in range(2):
                at = pl.ds(pl.multiple_of(slot * BLK + (core ^ odd) * TOK, TOK), TOK)
                if slot == 0:
                    ref = twin_ref if odd else mine_ref
                else:
                    ref = (odd_ref if odd else even_ref).at[slot - 1]
                rows_ref[at, :] = ref[:TOK, :]
                seg_ref[:, at] = ref[TOK:, :TOK].astype(f32)[:1]

    weights = lanes([wq_ref[...], wk_ref[...], wv_ref[...]])
    out = dot(rows_ref[...], weights, NN).astype(bf16)
    q_ref[...] = out[:, :PAIR]
    k_ref[...] = out[:, PAIR:2 * PAIR]
    v_ref[...] = out[:, 2 * PAIR:]


def project_rows(place, parts, wq, wk, wv):
    width, part = wq.shape
    length = BLK * (parts[2].shape[0] + 1)
    shape = jax.ShapeDtypeStruct((length, part), bf16)
    return pl.pallas_call(
        project_kernel,
        grid=(part // PAIR,),
        in_specs=[scalar()] + [full(x.shape) for x in parts] + [col(width)] * 3,
        out_specs=[col(length)] * 3 + [full((1, length)), full((length, width))],
        out_shape=[shape] * 3 + [jax.ShapeDtypeStruct((1, length), f32), jax.ShapeDtypeStruct((length, width), bf16)],
        compiler_params=params(),
        cost_estimate=cost(5),
        name="project",
    )(place, *parts, wq, wk, wv)


def pack_kernel(cols, kinds, *refs):
    *in_refs, out_ref, turn_ref = refs
    top = 0
    for ref, shares in zip(in_refs, kinds):
        tokens, count = out_ref.shape[2], ref.shape[1]
        for i in range(count // PAIR):
            turn_ref[i * PAIR:(i + 1) * PAIR, :] = ref[:tokens, i * PAIR:(i + 1) * PAIR].astype(f32).T
        size = count // (shares * cols)
        for c in range(cols):
            starts = [r * (count // shares) + c * size for r in range(shares)]
            rows = jnp.concatenate([turn_ref[a:a + size, :] for a in starts], axis=0)
            out_ref[c, top:top + shares * size, :] = rows.astype(bf16)
        top += shares * size


def pack(arrays, kinds, cols):
    tokens = arrays[0].shape[0]
    total = sum(x.shape[1] for x in arrays)
    return pl.pallas_call(
        functools.partial(pack_kernel, cols, kinds),
        in_specs=[whole()] * len(arrays),
        out_specs=whole(),
        out_shape=jax.ShapeDtypeStruct((cols, total // cols, tokens), bf16),
        scratch_shapes=[pltpu.VMEM((max(x.shape[1] for x in arrays), tokens), f32)],
        compiler_params=params(),
        cost_estimate=cost(3),
        name="pack",
    )(*arrays)


def layer_sums_kernel(rows, chunk, place_ref, pair_even_ref, pair_odd_ref, mine_ref, twin_ref, even_ref, odd_ref, part_ref,
                      earlier_ref, *out_refs):
    *out_refs, out_ref = out_refs
    me = 2 * place_ref[0] + place_ref[1]
    width = mine_ref.shape[1]
    features = part_ref.shape[1] - 2 * chunk
    half = width // 2
    down = up = out = small = 0.0
    for i in range(part_ref.shape[0] // 2):
        part = lanes([part_ref[me ^ (2 * i)], part_ref[me ^ (2 * i + 1)]])
        normed = jnp.concatenate([pair_even_ref[i, :, :width], pair_odd_ref[i, :, :width]], axis=0)
        branch = jnp.concatenate([pair_even_ref[i, :, width:], pair_odd_ref[i, :, width:]], axis=0)
        first, second = (even_ref.at[i - 1], odd_ref.at[i - 1]) if i else (mine_ref, twin_ref)
        attn = jnp.concatenate([first[:TOK, :], second[:TOK, :]], axis=0)
        down = down + dot(part[:chunk], branch, NN)
        out = out + dot(part[chunk:chunk + features], attn, NN)
        up = up + dot(part[chunk + features:], normed, NN)
        small = small + first[TOK:, :].astype(f32) + second[TOK:, :].astype(f32)
    up = up.T
    small = small[EXTRA - 4:]
    share, size, few = width // rows, chunk // rows, features // rows
    for r in range(rows):
        vectors = lanes([small[:, r * share:(r + 1) * share], jnp.zeros((4, chunk - share), f32)])
        pieces = [
            down[r * size:(r + 1) * size, :half], down[r * size:(r + 1) * size, half:],
            up[r * share:(r + 1) * share],
            out[r * few:(r + 1) * few, :half], out[r * few:(r + 1) * few, half:],
            vectors, jnp.zeros((EXTRA - 4, chunk), f32),
        ]
        out_ref[r] = jnp.concatenate(pieces, axis=0).astype(bf16)
    for k, ref in enumerate(out_refs):
        ref[...] = out_ref[place_ref[2] ^ k]


def layer_sums(place, pair, attn, parts, earlier, rows, chunk):
    width = attn[0].shape[1]
    features = parts.shape[1] - 2 * chunk
    height = (2 * chunk + 2 * features) // rows + width // rows + EXTRA
    return pl.pallas_call(
        functools.partial(layer_sums_kernel, rows, chunk),
        in_specs=[scalar()] + [whole()] * 7 + [unread()],
        out_specs=[whole()] * rows,
        out_shape=[jax.ShapeDtypeStruct((height, chunk), bf16)] * rows,
        scratch_shapes=[pltpu.VMEM((rows, height, chunk), bf16)],
        compiler_params=params(),
        cost_estimate=cost(6),
        name="layer_sums",
    )(place, *pair, *attn, parts, earlier)


def layer_unpack_kernel(cols, place_ref, even_ref, odd_ref, down_ref, up_ref, out_ref, small_ref):
    me = 2 * place_ref[0] + place_ref[1]
    half = down_ref.shape[1] // 2
    size, share, few = down_ref.shape[0] // cols, up_ref.shape[0], out_ref.shape[0] // cols
    chunk = up_ref.shape[1] // cols
    for ref, odd in ((even_ref, 0), (odd_ref, 1)):
        for i in range(cols // 2):
            spot = me ^ (2 * i + odd)
            part = ref[i].astype(f32)
            down_rows = pl.ds(pl.multiple_of(spot * size, 8), size)
            down_ref[down_rows, :half] = part[:size]
            down_ref[down_rows, half:] = part[size:2 * size]
            at = 2 * size + share
            up_ref[:, pl.ds(pl.multiple_of(spot * chunk, PAIR), chunk)] = part[2 * size:at]
            out_rows = pl.ds(pl.multiple_of(spot * few, 8), few)
            out_ref[out_rows, :half] = part[at:at + few]
            out_ref[out_rows, half:] = part[at + few:at + 2 * few]
            if i == 0 and not odd:
                small_ref[...] = part[at + 2 * few:at + 2 * few + 8, :share]


def layer_unpack(place, even, odd, rows, width, units):
    cols = 2 * even.shape[0]
    share = width // rows
    shapes = [(units // rows, width), (share, units), (share, width), (8, share)]
    return pl.pallas_call(
        functools.partial(layer_unpack_kernel, cols),
        in_specs=[scalar()] + [whole()] * 2,
        out_specs=[whole()] * 4,
        out_shape=[jax.ShapeDtypeStruct(x, f32) for x in shapes],
        compiler_params=params(),
        cost_estimate=cost(4),
        name="layer_unpack",
    )(place, even, odd)


def attn_sums_kernel(rows, place_ref, rows_ref, rel_ref, *refs):
    *out_refs, out_ref = refs[-rows - 1:]
    refs = refs[:-rows - 2]
    count = len(refs) // 2
    size = refs[0].shape[0]
    width, places = rows_ref.shape[1], rel_ref.shape[0]
    table_q = table_k = query = key = value = 0.0
    for j in range(count):
        rows_in = rows_ref[j * BLK:(j + 1) * BLK, :]
        q_ref, k_ref = refs[j], refs[count + j]
        query = query + dot(q_ref[:, places:], rows_in, NN)
        key = key + dot(k_ref[:, places:places + BLK], rows_in, NN)
        value = value + dot(k_ref[:, places + BLK:], rows_in, NN)
        table_k = table_k + q_ref[:, :places].astype(f32)
        table_q = table_q + k_ref[:, :places].astype(f32)
    query = query + dot(table_q.astype(bf16), rel_ref[...], NN)
    key = key + dot(table_k.astype(bf16), rel_ref[...], NN)
    pieces = [query, key, value]
    fill = -3 * size % PAIR
    if fill:
        pieces.append(jnp.zeros((fill, width), f32))
    full_sum = jnp.concatenate(pieces, axis=0).T
    share, spots = width // rows, places // rows
    wide = full_sum.shape[1]
    both = jnp.concatenate([table_q, table_k], axis=0)
    lines = 2 * size * spots // wide
    for r in range(rows):
        cut = both[:, r * spots:(r + 1) * spots]
        cut = lanes([cut[j * lines:(j + 1) * lines] for j in range(wide // spots)])
        out_ref[r] = jnp.concatenate([full_sum[r * share:(r + 1) * share], cut], axis=0).astype(bf16)
    for k, ref in enumerate(out_refs):
        ref[...] = out_ref[place_ref[2] ^ k]


def attn_sums(place, rows_in, rel, q_parts, k_parts, earlier, rows):
    size = q_parts[0].shape[0]
    width, places = rows_in.shape[1], rel.shape[0]
    wide = 3 * size + (-3 * size % PAIR)
    height = width // rows + 2 * size * (places // rows) // wide
    return pl.pallas_call(
        functools.partial(attn_sums_kernel, rows),
        in_specs=[scalar()] + [whole()] * (2 + len(q_parts) + len(k_parts)) + [unread()],
        out_specs=[whole()] * rows,
        out_shape=[jax.ShapeDtypeStruct((height, wide), bf16)] * rows,
        scratch_shapes=[pltpu.VMEM((rows, height, wide), bf16)],
        compiler_params=params(),
        cost_estimate=cost(5),
        name="attn_sums",
    )(place, rows_in, rel, *q_parts, *k_parts, earlier)


def attn_unpack_kernel(cols, spots, place_ref, even_ref, odd_ref, wq_ref, wk_ref, q_ref, k_ref, v_ref, rel_ref, all_ref,
                       tq_ref, tk_ref):
    me = 2 * place_ref[0] + place_ref[1]
    share, width = q_ref.shape
    size = width // cols
    for ref, odd in ((even_ref, 0), (odd_ref, 1)):
        for i in range(cols // 2):
            all_ref[me ^ (2 * i + odd)] = ref[i].astype(f32)
    wide = all_ref.shape[2]
    for c in range(cols):
        tail = all_ref[c, share:, :]
        tail = jnp.concatenate([tail[:, j * spots:(j + 1) * spots] for j in range(wide // spots)], axis=0)
        start = (c % 2) * width // 2 + (c // 2) * size
        spot = slice(start, start + size)
        for i, ref in enumerate((q_ref, k_ref, v_ref)):
            ref[:, spot] = all_ref[c, :share, i * size:(i + 1) * size]
        for i, ref in enumerate((tq_ref, tk_ref)):
            ref[spot, :] = tail[i * size:(i + 1) * size].astype(bf16)
    flip = flip_matrix(spots)
    turned_q = dot(tq_ref[...], flip, NN).astype(bf16)
    turned_k = dot(tk_ref[...], flip, NN).astype(bf16)
    across = (((0,), (1,)), ((), ()))
    rel_ref[...] = (dot(turned_q, wq_ref[...], across) + dot(turned_k, wk_ref[...], across)).astype(bf16)


def attn_unpack(place, even, odd, wq, wk, rows, places):
    cols = 2 * even.shape[0]
    width = wq.shape[0]
    share, spots = width // rows, places // rows
    shape = jax.ShapeDtypeStruct((share, width), f32)
    return pl.pallas_call(
        functools.partial(attn_unpack_kernel, cols, spots),
        in_specs=[scalar()] + [whole()] * 4,
        out_specs=[whole()] * 4,
        out_shape=[shape] * 3 + [jax.ShapeDtypeStruct((spots, width), bf16)],
        scratch_shapes=[pltpu.VMEM((cols,) + even.shape[1:], f32), pltpu.VMEM((width, spots), bf16),
                        pltpu.VMEM((width, spots), bf16)],
        compiler_params=params(),
        cost_estimate=cost(5),
        name="attn_unpack",
    )(place, even, odd, wq, wk)


HEADS = 12
EPSILON = 1e-07


def norm_forward(value, gain, shift):
    center = value - jnp.mean(value, axis=-1, keepdims=True)
    scaled = lax.rsqrt(jnp.mean(center * center, axis=-1, keepdims=True) + EPSILON)
    normed = center * scaled
    return (normed * gain + shift, normed, scaled)


def norm_backward(grad_out, normed, scaled, gain):
    grad_normed = grad_out * gain
    inner = grad_normed - jnp.mean(grad_normed, axis=-1, keepdims=True)
    inner = inner - normed * jnp.mean(grad_normed * normed, axis=-1, keepdims=True)
    return (scaled * inner, jnp.sum(grad_out * normed, axis=0), jnp.sum(grad_out, axis=0))


def gelu_exact(value):
    return jax.nn.gelu(value, approximate=False)


def mul(a, b, form=NN):
    return lax.dot_general(a, b, form, preferred_element_type=f32)


def swap(x, axis, k):
    return lax.ppermute(x, axis, [(i, i ^ k) for i in range(lax.axis_size(axis))])


def gather(x, *earlier):
    even = stack([x] + [swap(x, "seq", k) for k in range(2, lax.axis_size("seq"), 2)], *earlier)
    return even, swap(even, "seq", 1)


def gather_parts(x, *earlier):
    twin = swap(x, "seq", 1)
    even = stack([swap(x, "seq", k) for k in range(2, lax.axis_size("seq"), 2)], *earlier)
    return x, twin, even, swap(even, "seq", 1)


def deal_rows(parts):
    total = 0.0
    for k, part in enumerate(parts):
        total = total + (swap(part, "row", k) if k else part).astype(f32)
    return total.astype(bf16)


def deal_chips(parts):
    return [parts[0]] + [swap(part, "seq", 2 * k) for k, part in enumerate(parts) if k]


def in_order(parts, chip):
    out = jnp.zeros((len(parts),) + parts[0].shape, parts[0].dtype)
    for k, part in enumerate(parts):
        out = lax.dynamic_update_slice_in_dim(out, part[None], chip ^ k, 0)
    return out.reshape((-1,) + parts[0].shape[1:])


def reduced(g):
    part = lax.psum_scatter(g.astype(bf16), "row", scatter_dimension=0, tiled=True)
    return lax.psum(part, "seq").astype(f32)


def on_device(
    hidden, segments, rel_embed, query_weight, key_weight, value_weight, output_weight, up_weight, down_weight,
    norm1_gain, norm1_bias, norm2_gain, norm2_bias, cotangent,
):
    tokens, width = hidden.shape[1:]
    places = rel_embed.shape[0]
    units = up_weight.shape[1]
    part = width // 2
    scale = 1.0 / math.sqrt(3.0 * (width // HEADS))
    inputs = hidden[0]
    cols, rows = lax.axis_size("seq"), lax.axis_size("row")
    chip, core = lax.axis_index("seq") // 2, lax.axis_index("seq") % 2
    row = lax.axis_index("row")
    place = jnp.stack([chip, core, row]).astype(jnp.int32)
    share = width // rows
    chunk = units // cols
    dealt = (units // (rows * cols)) % 16 == 0 and places // rows == TOK

    def core_cols(w):
        return lax.dynamic_slice_in_dim(w, core * part, part, 1)

    def meet(x):
        mine = lax.dynamic_index_in_dim(x, core, 0, keepdims=False)
        other = swap(lax.dynamic_index_in_dim(x, 1 - core, 0, keepdims=False), "seq", 1)
        return jnp.where(core == 0, jnp.concatenate([mine, other], axis=-1), jnp.concatenate([other, mine], axis=-1))

    half_q, half_k, half_v = core_cols(query_weight), core_cols(key_weight), core_cols(value_weight)
    half_out = lax.dynamic_slice_in_dim(output_weight, core * part, part, 0)
    rel_flip = mul(flip_matrix(places), rel_embed).astype(bf16)
    qr = mul(rel_flip, half_q).astype(bf16)
    kr = mul(rel_flip, half_k).astype(bf16)
    seg_rows = jnp.pad(segments.astype(bf16), ((0, EXTRA - 1), (0, width - tokens)))
    in_parts = gather_parts(jnp.concatenate([inputs, seg_rows], axis=0), qr, kr)
    q, k, v, row_segs, row_in = project_rows(place, in_parts, half_q, half_k, half_v)
    own_segs = row_segs[0, :BLK].reshape(BLK, 1)

    probs, ctx_half = forward_attention(place, q, k, v, kr, qr, own_segs, row_segs, scale)
    ctx = meet(ctx_half)

    ctx_low = ctx[:tokens].astype(bf16)
    h1 = inputs.astype(f32) + mul(ctx_low, output_weight)
    normed1, unit1, scaled1 = norm_forward(h1, norm1_gain, norm1_bias)
    normed1_low = normed1.astype(bf16)
    inner = mul(normed1_low, up_weight)
    active, gelu_back = jax.vjp(gelu_exact, inner)
    active_low = active.astype(bf16)
    result, unit2, scaled2 = norm_forward(normed1 + mul(active_low, down_weight), norm2_gain, norm2_bias)
    output = result.astype(bf16)[None]
    cot = cotangent[0].astype(f32)
    d_h2, g_gain2, g_bias2 = norm_backward(cot, unit2, scaled2, norm2_gain)
    d_branch = d_h2.astype(bf16)
    d_inner = gelu_back(mul(d_branch, down_weight, NT))[0].astype(bf16)
    d_normed1 = d_h2 + mul(d_inner, up_weight, NT)
    d_h1, g_gain1, g_bias1 = norm_backward(d_normed1, unit1, scaled1, norm1_gain)
    d_attn = d_h1.astype(bf16)
    vectors = jnp.stack([g_gain1, g_bias1, g_gain2, g_bias2])
    attn_pay = attn_out(d_attn, output_weight, ctx, vectors)
    parts = pack([active_low, ctx, d_inner], [rows, rows, 1], cols) if dealt else attn_pay
    twin = swap(attn_pay, "seq", 1)
    dq_half, *q_table = query_grads(place, probs, attn_pay, twin, half_out, ctx_half, v, q, k, kr, parts, scale)
    even = stack([swap(attn_pay, "seq", i) for i in range(2, cols, 2)], dq_half)
    attn = attn_pay, twin, even, swap(even, "seq", 1)
    dk_half, dv_half, *k_table = key_grads(
        place, k, v, q, qr, kr, own_segs, row_segs, attn, half_out, dq_half, scale
    )
    d_own = meet(jnp.concatenate([dq_half, dk_half, dv_half], axis=1))
    dq, dk, dv = (d_own[i * tokens:(i + 1) * tokens] for i in range(3))
    grad_in = d_h1 + mul(dq, query_weight, NT) + mul(dk, key_weight, NT) + mul(dv, value_weight, NT)

    if dealt:
        q_parts = deal_chips(q_table)
        pair = gather(after(jnp.concatenate([normed1_low, d_branch], axis=1), dq_half), dk_half)
        parts = lax.all_to_all(parts, "seq", 0, 0, tiled=True)
        k_parts = deal_chips([after(x, parts, pair[0]) if i == 1 else x for i, x in enumerate(k_table)])
        layer_part = layer_sums(place, pair, attn, parts, dk_half, rows, chunk)
        layer = deal_rows(layer_part)
        g_down, g_up, g_output, small = layer_unpack(place, *gather(layer), rows, width, units)
        attn_part = attn_sums(place, row_in, rel_flip, q_parts, k_parts, layer_part[0], rows)
        sums = deal_rows(attn_part)
        g_query, g_key, g_value, g_rel = attn_unpack(place, *gather(sums), query_weight, key_weight, rows, places)
        blocks = [g_rel] + [swap(g_rel, "row", k) for k in range(1, rows)]
        out = jnp.zeros((rows,) + g_rel.shape, bf16)
        for k, block in enumerate(blocks):
            out = lax.dynamic_update_slice_in_dim(out, block[None], rows - 1 - (row ^ k), 0)
        g_rel = out.reshape(places, width).astype(f32)
    else:
        small = jnp.stack([reduced(x) for x in (g_gain1, g_bias1, g_gain2, g_bias2)])
        g_down = reduced(mul(active_low, d_branch, TN))
        g_up = reduced(mul(normed1_low, d_inner, TN))
        g_output = reduced(mul(ctx_low, d_attn, TN))
        across = (((0,), (1,)), ((), ()))
        d_kr, d_qr = (in_order(x, chip)[:, :places] for x in (q_table, k_table))
        placed = lambda g: lax.dynamic_update_slice_in_dim(jnp.zeros((width, width), f32), g, core * part, 1)
        g_query = reduced(mul(inputs, dq, TN) + placed(mul(rel_flip, d_qr, across)))
        g_key = reduced(mul(inputs, dk, TN) + placed(mul(rel_flip, d_kr, across)))
        g_value = reduced(mul(inputs, dv, TN))
        g_rel = mul(d_qr, half_q, across) + mul(d_kr, half_k, across)
        g_rel = lax.psum(mul(flip_matrix(places), g_rel.astype(bf16)).astype(bf16), ("seq", "row")).astype(f32)

    return (
        output, grad_in.astype(bf16)[None], g_query, g_key, g_value, g_output, g_up, g_down,
        small[0], small[1], small[2], small[3], g_rel,
    )


def solution(mesh):
    split = P("row", "seq", None)
    return jax.shard_map(
        on_device,
        mesh=mesh,
        in_specs=(split, P("row", "seq")) + (P(),) * 11 + (split,),
        out_specs=(split, split) + (P("row", None),) * 6 + (P("row"),) * 4 + (P(),),
        check_vma=False,
    )
```

```python
import functools, math
import jax, jax.numpy as jnp
from jax import lax
from jax.experimental import pallas as pl
from jax.experimental.pallas import tpu as pltpu
from jax.sharding import PartitionSpec as P

BLK = 256
TOK = 128
PAIR = 128
EXTRA = 16
COST = 1e6
EPSILON = 1e-07
NT = (((1,), (1,)), ((), ()))
NN = (((1,), (0,)), ((), ()))
TN = (((0,), (0,)), ((), ()))
bf16 = jnp.bfloat16
f32 = jnp.float32


def dot(a, b, form):
    return lax.dot_general(a, b, form, preferred_element_type=f32)


def lanes(parts):
    return jnp.concatenate(parts, axis=1)


def half_masks(x):
    lane = lax.broadcasted_iota(jnp.int32, x.shape, 1)
    low = lane < PAIR // 2
    zero = jnp.zeros_like(x)
    return jnp.where(low, x, zero), jnp.where(low, zero, x)


def join_heads(stacked, rows):
    lane = lax.broadcasted_iota(jnp.int32, (rows, PAIR), 1)
    return jnp.where(lane < PAIR // 2, stacked[:rows], stacked[rows:])


def block_start(chip, slot):
    return pl.multiple_of((chip ^ slot) * BLK, BLK)


def fill_table(out_ref, flip_ref, start):
    places = flip_ref.shape[0]
    low = jnp.broadcast_to(flip_ref[0:1, :], (BLK, PAIR))
    high = jnp.broadcast_to(flip_ref[places - 1:places, :], (BLK, PAIR))
    for b in range(out_ref.shape[0] // BLK):
        out_ref[b * BLK:(b + 1) * BLK, :] = jnp.where(b * BLK < start, low, high)
    out_ref[pl.ds(pl.multiple_of(start, BLK), places), :] = flip_ref[...]


def fill_scores(chip, own_ref, all_ref, near_ref, far_ref, s_ref, n_ref, length):
    wide = length + BLK
    own = jnp.concatenate(half_masks(own_ref[...]), axis=0)
    ext = dot(own, near_ref[...], NT)
    for h in range(2):
        moved = pltpu.roll(ext[h * BLK:(h + 1) * BLK], wide - (BLK - 1), 1, stride=1, stride_axis=0)
        n_ref[h] = moved[:, :length]
    for slot in range(length // BLK):
        cols = slice(slot * BLK, (slot + 1) * BLK)
        blk = all_ref[cols, :]
        both = jnp.concatenate(half_masks(blk), axis=0)
        start = block_start(chip, slot)
        win = far_ref[pl.ds(pl.multiple_of(length - BLK - start, BLK), 2 * BLK), :]
        back = dot(both, win, NT)
        direct = dot(own, blk, NT)
        for h in range(2):
            rows = slice(h * BLK, (h + 1) * BLK)
            moved = pltpu.roll(back[rows], BLK + 1, 1, stride=1, stride_axis=0)[:, :BLK]
            s_ref[h, :, cols] = direct[rows] + moved.T + n_ref[h, :, pl.ds(start, BLK)]


def far_start(chip, length):
    return length - BLK - chip * BLK


def forward_kernel(scale, length, place_ref, q_ref, k_ref, v_ref, near_ref, far_ref, segq_ref, segk_ref,
                   p_ref, out_ref, s_ref, n_ref, near_tab, far_tab):
    chip = place_ref[0]
    fill_table(near_tab, near_ref, chip * BLK)
    fill_table(far_tab, far_ref, far_start(chip, length))
    fill_scores(chip, q_ref, k_ref, near_tab, far_tab, s_ref, n_ref, length)
    allowed = segq_ref[...] == segk_ref[...]
    stats = []
    for h in range(2):
        logits = jnp.where(allowed, s_ref[h] * scale, -1e30)
        best = jnp.max(logits, axis=1, keepdims=True)
        weights = jnp.exp(logits - best)
        total = jnp.sum(weights, axis=1, keepdims=True)
        p_ref[h] = (weights * (1.0 / total)).astype(bf16)
        stats.append(best + jnp.log(total))
    stacked = jnp.concatenate([p_ref[0], p_ref[1]], axis=0)
    ctx = join_heads(dot(stacked, v_ref[...], NN), BLK)
    lane = lax.broadcasted_iota(jnp.int32, (TOK, PAIR), 1)
    for c in range(2):
        rows = slice(c * TOK, (c + 1) * TOK)
        out_ref[c, :TOK, :] = ctx[rows]
        out_ref[c, TOK:, :] = jnp.where(lane == 0, stats[0][rows], stats[1][rows]).T[:8]


def flip_matrix(count):
    r = lax.broadcasted_iota(jnp.int32, (count, count), 0)
    c = lax.broadcasted_iota(jnp.int32, (count, count), 1)
    return jnp.where(r + c == count - 1, 1.0, 0.0).astype(bf16)


def fold_table(grad, start, places, fold_ref):
    place = lax.broadcasted_iota(jnp.int32, grad.shape, 1)
    low = jnp.sum(jnp.where(place < start, grad, 0.0), axis=1, keepdims=True)
    high = jnp.sum(jnp.where(place >= start + places, grad, 0.0), axis=1, keepdims=True)
    fold_ref[...] = grad
    table = fold_ref[:, pl.ds(pl.multiple_of(start, BLK), places)]
    spot = lax.broadcasted_iota(jnp.int32, table.shape, 1)
    return table + jnp.where(spot == 0, low, 0.0) + jnp.where(spot == places - 1, high, 0.0)


def grads_tail(scale, length, places, chip, ds_ref, own_ref, all_ref, near_ref, table_ref, wide_ref, down_ref, fold_ref, n_ref):
    flip = flip_matrix(BLK)
    rows = pair_rows()
    for h in range(2):
        back = dot(flip, ds_ref[h], NN)
        down_ref[h * BLK:(h + 1) * BLK, :] = back.astype(bf16)
        for slot in range(length // BLK):
            n_ref[h, :, pl.ds(block_start(chip, slot), BLK)] = back[:, slot * BLK:(slot + 1) * BLK]
        padded = lanes([n_ref[h], jnp.zeros((BLK, BLK), f32)])
        wide_ref[h * BLK:(h + 1) * BLK, :] = pltpu.roll(padded, 0, 1, stride=1, stride_axis=0).astype(bf16)
    own_grad = dot(down_ref[...], all_ref[...], NN) + dot(wide_ref[...], near_ref[...], NN)
    own_grad = (join_heads(own_grad, BLK) * scale).astype(bf16)
    table_ref[rows, places:places + BLK] = dot(own_grad, flip, TN).astype(bf16)
    own_grad = dot(flip, own_grad, NN).astype(bf16)
    own = dot(flip, own_ref[...], NN).astype(bf16)
    own = jnp.concatenate(half_masks(own), axis=0)
    near_grad = dot(own, wide_ref[...], TN) * scale
    table_ref[rows, :places] = fold_table(near_grad, chip * BLK, places, fold_ref).astype(bf16)
    return own_grad


def pair_rows():
    return pl.ds(pl.multiple_of(pl.program_id(0) * PAIR, PAIR), PAIR)


def deal_table(chip, table_ref, out_refs):
    @pl.when(pl.program_id(0) == pl.num_programs(0) - 1)
    def _():
        for k, ref in enumerate(out_refs):
            size = ref.shape[0]
            ref[...] = table_ref[pl.ds(pl.multiple_of((chip ^ k) * size, EXTRA), size), :]


def split_tokens(out_ref, value):
    for c in range(2):
        out_ref[c] = value[c * TOK:(c + 1) * TOK]


def query_grad_kernel(scale, length, chips, place_ref, p_ref, mine_ref, twin_ref, out_weight_ref, ctx_ref, v_ref, q_ref, k_ref,
                      near_ref, earlier_ref, dq_ref, *refs):
    out_refs, (near_tab, dctx_ref, table_ref, ds_ref, *scratch) = refs[:chips], refs[chips:]
    chip, core = place_ref[0], place_ref[1]
    places = near_ref.shape[0]
    fill_table(near_tab, near_ref, chip * BLK)
    for ref, at in ((mine_ref, core), (twin_ref, 1 - core)):
        rows = pl.ds(pl.multiple_of(at * TOK, TOK), TOK)
        dctx_ref[rows, :] = dot(ref[:TOK, :], out_weight_ref[...], NT).astype(bf16)
    dctx = jnp.concatenate(half_masks(dctx_ref[...]), axis=0)
    dprob = dot(dctx, v_ref[...], NT)
    ctx = jnp.concatenate([ctx_ref[0, :TOK, :], ctx_ref[1, :TOK, :]], axis=0)
    for h in range(2):
        rows = slice(h * BLK, (h + 1) * BLK)
        row_dot = jnp.sum(dctx[rows].astype(f32) * ctx, axis=1, keepdims=True)
        ds_ref[h] = (p_ref[h].astype(f32) * (dprob[rows] - row_dot)).astype(bf16)
    dq = grads_tail(scale, length, places, chip, ds_ref, q_ref, k_ref, near_tab, table_ref, *scratch)
    split_tokens(dq_ref, dq)
    deal_table(chip, table_ref, out_refs)


def key_grad_kernel(scale, length, pairs, chips, place_ref, k_ref, v_ref, q_ref, near_ref, far_ref, segk_ref, segq_ref,
                    mine_ref, twin_ref, even_ref, odd_ref, out_weight_ref, earlier_ref, dk_ref, dv_ref, *refs):
    out_refs, refs = refs[:chips], refs[chips:]
    s_ref, near_tab, far_tab, dctx_ref, p_ref, stat_ref, table_ref, ds_ref, *scratch = refs
    chip, core = place_ref[0], place_ref[1]
    places = near_ref.shape[0]
    fill_table(near_tab, near_ref, chip * BLK)
    fill_table(far_tab, far_ref, far_start(chip, length))
    fill_scores(chip, k_ref, q_ref, near_tab, far_tab, s_ref, scratch[-1], length)
    stat_cols = pl.ds(pl.multiple_of((core * pairs + pl.program_id(0)) * PAIR, PAIR), PAIR)
    for slot in range(length // BLK):
        for odd in range(2):
            at = pl.ds(pl.multiple_of(slot * BLK + (core ^ odd) * TOK, TOK), TOK)
            if slot == 0:
                ref = twin_ref if odd else mine_ref
            else:
                ref = (odd_ref if odd else even_ref).at[slot - 1]
            dctx_ref[at, :] = dot(ref[:TOK, :], out_weight_ref[...], NT).astype(bf16)
            stat_ref[:, at] = ref[TOK:, stat_cols].astype(f32)
    merged = [stat_ref[3 * j:3 * j + 1] + stat_ref[3 * j + 1:3 * j + 2] + stat_ref[3 * j + 2:3 * j + 3] for j in range(4)]
    allowed = segk_ref[...] == segq_ref[...]
    dctx = dctx_ref[...]
    vals = jnp.concatenate(half_masks(v_ref[...]), axis=0)
    dprob = dot(vals, dctx, NT)
    for h in range(2):
        rows = slice(h * BLK, (h + 1) * BLK)
        probs = jnp.where(allowed, jnp.exp(s_ref[h] * scale - merged[h]), 0.0)
        p_ref[rows, :] = probs.astype(bf16)
        ds_ref[h] = (probs * (dprob[rows] - merged[2 + h])).astype(bf16)
    dv = join_heads(dot(p_ref[...], dctx, NN), BLK)
    split_tokens(dv_ref, dv.astype(bf16))
    table_ref[pair_rows(), places + BLK:] = dv.T.astype(bf16)
    dk = grads_tail(scale, length, places, chip, ds_ref, k_ref, q_ref, near_tab, table_ref, *scratch)
    split_tokens(dk_ref, dk)
    deal_table(chip, table_ref, out_refs)


def col(rows):
    return pl.BlockSpec((rows, PAIR), lambda p: (0, p))


def full(shape):
    return pl.BlockSpec(shape, lambda p: (0,) * len(shape))


def whole():
    return pl.BlockSpec(memory_space=pltpu.VMEM)


def scalar():
    return pl.BlockSpec(memory_space=pltpu.SMEM)


def unread():
    return pl.BlockSpec(memory_space=pl.ANY)


def params():
    return pltpu.CompilerParams(vmem_limit_bytes=56 * 1024 * 1024)


def cost(microseconds):
    return pl.CostEstimate(flops=int(microseconds * COST), bytes_accessed=0, transcendentals=0)


def after(x, *earlier):
    def kernel(*refs):
        pass

    return pl.pallas_call(
        kernel,
        in_specs=[unread()] * (1 + len(earlier)),
        out_specs=unread(),
        out_shape=jax.ShapeDtypeStruct(x.shape, x.dtype),
        input_output_aliases={0: 0},
        cost_estimate=cost(0.1),
        name="after",
    )(x, *earlier)


def stack_kernel(count, *refs):
    for i in range(count):
        refs[-1][i] = refs[i][...]


def stack(arrays, *earlier):
    count = len(arrays)
    return pl.pallas_call(
        functools.partial(stack_kernel, count),
        in_specs=[whole()] * count + [unread()] * len(earlier),
        out_specs=whole(),
        out_shape=jax.ShapeDtypeStruct((count,) + arrays[0].shape, arrays[0].dtype),
        compiler_params=params(),
        cost_estimate=cost(1),
        name="stack",
    )(*arrays, *earlier)


def sum_kernel(count, *refs):
    total = 0.0
    for ref in refs[:count]:
        total = total + ref[...].astype(f32)
    refs[-1][...] = total.astype(bf16)


def sum_arrays(arrays, *earlier):
    count = len(arrays)
    return pl.pallas_call(
        functools.partial(sum_kernel, count),
        in_specs=[whole()] * count + [unread()] * len(earlier),
        out_specs=whole(),
        out_shape=jax.ShapeDtypeStruct(arrays[0].shape, bf16),
        compiler_params=params(),
        cost_estimate=cost(1),
        name="sum_rows",
    )(*arrays, *earlier)


def join_kernel(place_ref, *refs):
    *refs, _, _, out_ref = refs
    size = refs[0].shape[0]
    for k, ref in enumerate(refs):
        spot = len(refs) - 1 - (place_ref[2] ^ k)
        out_ref[pl.ds(pl.multiple_of(spot * size, size), size), :] = ref[...].astype(f32)


def join_rows(place, blocks, *earlier):
    size, width = blocks[0].shape
    return pl.pallas_call(
        join_kernel,
        in_specs=[scalar()] + [whole()] * len(blocks) + [unread()] * 2,
        out_specs=whole(),
        out_shape=jax.ShapeDtypeStruct((len(blocks) * size, width), f32),
        compiler_params=params(),
        cost_estimate=cost(1),
        name="join_rows",
    )(place, *blocks, *earlier)


def table_scratch(length):
    return pltpu.VMEM((length + BLK, PAIR), bf16)


def probs_block(length):
    return pl.BlockSpec((2, BLK, length), lambda p: (p, 0, 0))


def token_block():
    return pl.BlockSpec((2, TOK, PAIR), lambda p: (0, 0, p))


def forward_attention(place, q, k, v, near, far, seg_q, seg_k, scale):
    length, width = k.shape
    places = near.shape[0]
    pairs = width // PAIR
    return pl.pallas_call(
        functools.partial(forward_kernel, scale, length),
        grid=(pairs,),
        in_specs=[scalar(), col(BLK), col(length), col(length), col(places), col(places), full((BLK, 1)), full((1, length))],
        out_specs=[probs_block(length), pl.BlockSpec((2, TOK + 8, PAIR), lambda p: (0, 0, p))],
        out_shape=[
            jax.ShapeDtypeStruct((2 * pairs, BLK, length), bf16),
            jax.ShapeDtypeStruct((2, TOK + 8, width), f32),
        ],
        scratch_shapes=[pltpu.VMEM((2, BLK, length), f32)] * 2 + [table_scratch(length)] * 2,
        compiler_params=params(),
        cost_estimate=cost(14),
        name="attend",
    )(place, q, k, v, near, far, seg_q, seg_k)


def grad_scratch(length):
    return [
        pltpu.VMEM((2, BLK, length), bf16),
        pltpu.VMEM((2 * BLK, length + BLK), bf16),
        pltpu.VMEM((2 * BLK, length), bf16),
        pltpu.VMEM((PAIR, length + BLK), f32),
        pltpu.VMEM((2, BLK, length), f32),
    ]


def query_grads(place, p, mine, twin, out_weight, ctx, v, q, k, near, earlier, scale):
    length, width = k.shape
    places = near.shape[0]
    chips = length // BLK
    table = jax.ShapeDtypeStruct((width // chips, places + BLK), bf16)
    return pl.pallas_call(
        functools.partial(query_grad_kernel, scale, length, chips),
        grid=(width // PAIR,),
        in_specs=[scalar(), probs_block(length), full(mine.shape), full(twin.shape),
                  pl.BlockSpec((PAIR, out_weight.shape[1]), lambda p: (p, 0)),
                  pl.BlockSpec((2, TOK + 8, PAIR), lambda p: (0, 0, p)), col(length), col(BLK), col(length), col(places),
                  unread()],
        out_specs=[token_block()] + [full(table.shape)] * chips,
        out_shape=[jax.ShapeDtypeStruct((2, TOK, width), bf16)] + [table] * chips,
        scratch_shapes=[table_scratch(length), pltpu.VMEM((BLK, PAIR), bf16), pltpu.VMEM((width, places + BLK), bf16)]
        + grad_scratch(length),
        compiler_params=params(),
        cost_estimate=cost(1),
        name="query_grads",
    )(place, p, mine, twin, out_weight, ctx, v, q, k, near, earlier)


def key_grads(place, k, v, q, near, far, seg_k, seg_q, attn, out_weight, earlier, scale):
    length, width = q.shape
    places = near.shape[0]
    pairs = width // PAIR
    chips = length // BLK
    table = jax.ShapeDtypeStruct((width // chips, places + 2 * BLK), bf16)
    return pl.pallas_call(
        functools.partial(key_grad_kernel, scale, length, pairs, chips),
        grid=(pairs,),
        in_specs=[scalar(), col(BLK), col(BLK), col(length), col(places), col(places), full((BLK, 1)), full((1, length))]
        + [full(x.shape) for x in attn]
        + [pl.BlockSpec((PAIR, out_weight.shape[1]), lambda p: (p, 0)), unread()],
        out_specs=[token_block(), token_block()] + [full(table.shape)] * chips,
        out_shape=[jax.ShapeDtypeStruct((2, TOK, width), bf16)] * 2 + [table] * chips,
        scratch_shapes=[pltpu.VMEM((2, BLK, length), f32), table_scratch(length), table_scratch(length),
                        pltpu.VMEM((length, PAIR), bf16), pltpu.VMEM((2 * BLK, length), bf16),
                        pltpu.VMEM((EXTRA, length), f32), pltpu.VMEM((width, places + 2 * BLK), bf16)]
        + grad_scratch(length),
        compiler_params=params(),
        cost_estimate=cost(1),
        name="key_grads",
    )(place, k, v, q, near, far, seg_k, seg_q, *attn, out_weight, earlier)


def project_kernel(place_ref, mine_ref, twin_ref, even_ref, odd_ref, wq_ref, wk_ref, wv_ref, q_ref, k_ref, v_ref, seg_ref,
                   rows_ref):
    core = place_ref[1]
    count = even_ref.shape[0] + 1

    @pl.when(pl.program_id(0) == 0)
    def _():
        for slot in range(count):
            for odd in range(2):
                at = pl.ds(pl.multiple_of(slot * BLK + (core ^ odd) * TOK, TOK), TOK)
                if slot == 0:
                    ref = twin_ref if odd else mine_ref
                else:
                    ref = (odd_ref if odd else even_ref).at[slot - 1]
                rows_ref[at, :] = ref[:TOK, :]
                seg_ref[:, at] = ref[TOK:, :TOK].astype(f32)[:1]

    weights = lanes([wq_ref[...], wk_ref[...], wv_ref[...]])
    out = dot(rows_ref[...], weights, NN).astype(bf16)
    q_ref[...] = out[:, :PAIR]
    k_ref[...] = out[:, PAIR:2 * PAIR]
    v_ref[...] = out[:, 2 * PAIR:]


def project_rows(place, parts, wq, wk, wv):
    width, part = wq.shape
    length = BLK * (parts[2].shape[0] + 1)
    shape = jax.ShapeDtypeStruct((length, part), bf16)
    return pl.pallas_call(
        project_kernel,
        grid=(part // PAIR,),
        in_specs=[scalar()] + [full(x.shape) for x in parts] + [col(width)] * 3,
        out_specs=[col(length)] * 3 + [full((1, length)), full((length, width))],
        out_shape=[shape] * 3 + [jax.ShapeDtypeStruct((1, length), f32), jax.ShapeDtypeStruct((length, width), bf16)],
        compiler_params=params(),
        cost_estimate=cost(5),
        name="project",
    )(place, *parts, wq, wk, wv)


def mean(x):
    return jnp.mean(x, axis=-1, keepdims=True)


def norm_forward(value):
    center = value - mean(value)
    scaled = lax.rsqrt(mean(center * center) + EPSILON)
    return center * scaled, scaled


def norm_backward(grad_out, normed, scaled, gain):
    grad_normed = grad_out * gain
    inner = grad_normed - mean(grad_normed) - normed * mean(grad_normed * normed)
    return scaled * inner, jnp.sum(grad_out * normed, axis=0, keepdims=True), jnp.sum(grad_out, axis=0, keepdims=True)


def turn(turn_ref, at, value):
    for i in range(value.shape[1] // PAIR):
        turn_ref[pl.ds(pl.multiple_of(at + i * PAIR, PAIR), PAIR), :] = value[:, i * PAIR:(i + 1) * PAIR].T


def pack(out_ref, top, turn_ref, count, shares, cols):
    size = count // (shares * cols)
    for c in range(cols):
        starts = [r * (count // shares) + c * size for r in range(shares)]
        rows = jnp.concatenate([turn_ref[a:a + size, :] for a in starts], axis=0)
        out_ref[c, top:top + shares * size, :] = rows.astype(bf16)


def layer_forward_kernel(cols, rows, in_ref, ctx_ref, out_weight_ref, up_ref, down_ref, cot_ref, gain1_ref, bias1_ref,
                         gain2_ref, bias2_ref, output_ref, pair_ref, active_ref, slope_ref, unit_ref, scaled_ref,
                         d_h2_ref, vec_ref, part_ref, normed_ref, sum_ref, turn_ref):
    step = pl.program_id(0)
    tokens, width = in_ref.shape
    chunk = up_ref.shape[1]

    @pl.when(step == 0)
    def _():
        h1 = in_ref[...].astype(f32) + dot(ctx_ref[:tokens, :].astype(bf16), out_weight_ref[...], NN)
        unit, scaled = norm_forward(h1)
        unit_ref[...] = unit
        scaled_ref[...] = jnp.broadcast_to(scaled, scaled_ref.shape)
        normed = unit * gain1_ref[...] + bias1_ref[...]
        normed_ref[...] = normed.astype(bf16)
        pair_ref[:, :width] = normed.astype(bf16)
        sum_ref[...] = normed

    inner = dot(normed_ref[...], up_ref[...], NN)
    upper = 0.5 * (1.0 + lax.erf(inner * math.sqrt(0.5)))
    slope_ref[...] = upper + inner * jnp.exp(-0.5 * inner * inner) * (1.0 / math.sqrt(2.0 * math.pi))
    active = (inner * upper).astype(bf16)
    active_ref[...] = active
    sum_ref[...] += dot(active, down_ref[...], NN)
    if part_ref is not None:
        turn(turn_ref, step * chunk, active.astype(f32))

    @pl.when(step == pl.num_programs(0) - 1)
    def _():
        unit, scaled = norm_forward(sum_ref[...])
        output_ref[...] = (unit * gain2_ref[...] + bias2_ref[...]).astype(bf16)
        d_h2, g_gain, g_bias = norm_backward(cot_ref[...].astype(f32), unit, scaled, gain2_ref[...])
        d_h2_ref[...] = d_h2
        pair_ref[:, width:] = d_h2.astype(bf16)
        vec_ref[...] = jnp.concatenate([g_gain, g_bias] * 4, axis=0)
        if part_ref is not None:
            units = turn_ref.shape[0]
            pack(part_ref, 0, turn_ref, units, rows, cols)
            turn(turn_ref, 0, ctx_ref[:tokens, :])
            pack(part_ref, units // cols, turn_ref, width, rows, cols)


def step_cols(rows, chunk):
    return pl.BlockSpec((rows, chunk), lambda i: (0, i))


def step_rows(chunk, cols):
    return pl.BlockSpec((chunk, cols), lambda i: (i, 0))


def layer_forward(inputs, ctx, out_weight, up, down, cot, vectors, cols, rows, dealt):
    tokens, width = inputs.shape
    units = up.shape[1]
    chunk = width
    square = (tokens, width)
    shapes = [(square, bf16), ((tokens, 2 * width), bf16), ((tokens, units), bf16), ((tokens, units), f32), (square, f32),
              ((tokens, PAIR), f32), (square, f32), ((8, width), f32)]
    specs = [full(square), full((tokens, 2 * width)), step_cols(tokens, chunk), step_cols(tokens, chunk), full(square),
             full((tokens, PAIR)), full(square), full((8, width))]
    kernel = functools.partial(layer_forward_kernel, cols, rows)
    if dealt:
        shapes.append(((cols, (units + width) // cols, tokens), bf16))
        specs.append(full(shapes[-1][0]))
    else:
        kernel = lambda *refs: layer_forward_kernel(cols, rows, *refs[:-3], None, *refs[-3:])
    return pl.pallas_call(
        kernel,
        grid=(units // chunk,),
        in_specs=[full(square), full(ctx.shape), full(out_weight.shape), step_cols(width, chunk), step_rows(chunk, width),
                  full(square)] + [full((1, width))] * 4,
        out_specs=specs,
        out_shape=[jax.ShapeDtypeStruct(*x) for x in shapes],
        scratch_shapes=[pltpu.VMEM(square, bf16), pltpu.VMEM(square, f32), pltpu.VMEM((units, tokens), f32)],
        compiler_params=params(),
        cost_estimate=cost(1),
        name="layer_forward",
    )(inputs, ctx, out_weight, up, down, cot, *(x.reshape(1, width) for x in vectors))


def layer_backward_kernel(cols, pair_ref, slope_ref, down_ref, up_ref, d_h2_ref, unit_ref, scaled_ref, gain1_ref,
                          out_weight_ref, ctx_ref, vec_ref, d_h1_ref, pay_ref, din_ref, part_ref, sum_ref, turn_ref):
    step = pl.program_id(0)
    tokens, width = d_h2_ref.shape
    chunk = up_ref.shape[1]
    d_inner = (dot(pair_ref[:, width:], down_ref[...], NT) * slope_ref[...]).astype(bf16)
    din_ref[...] = d_inner
    part = dot(d_inner, up_ref[...], NT)
    if part_ref is not None:
        turn(turn_ref, step * chunk, d_inner.astype(f32))

    @pl.when(step == 0)
    def _():
        sum_ref[...] = d_h2_ref[...] + part

    @pl.when(step > 0)
    def _():
        sum_ref[...] += part

    @pl.when(step == pl.num_programs(0) - 1)
    def _():
        d_h1, g_gain, g_bias = norm_backward(sum_ref[...], unit_ref[...], scaled_ref[:, :1], gain1_ref[...])
        d_h1_ref[...] = d_h1
        d_attn = d_h1.astype(bf16)
        pay_ref[:tokens, :] = d_attn
        vectors = jnp.concatenate([g_gain, g_bias, vec_ref[:2]], axis=0)
        half = PAIR // 2
        for p in range(width // PAIR):
            at = slice(p * PAIR, (p + 1) * PAIR)
            d_ctx = dot(d_attn, out_weight_ref[at, :], NT).astype(bf16)
            turned = (d_ctx.astype(f32) * ctx_ref[:tokens, at]).T
            rows = [ctx_ref[tokens:tokens + 1, at], ctx_ref[tokens + 1:tokens + 2, at],
                    jnp.sum(turned[:half], axis=0, keepdims=True), jnp.sum(turned[half:], axis=0, keepdims=True)]
            pieces = []
            for value in rows:
                for _ in range(3):
                    piece = value.astype(bf16).astype(f32)
                    pieces.append(piece)
                    value = value - piece
            pieces.append(vectors[:, at])
            pay_ref[tokens:, at] = jnp.concatenate(pieces, axis=0).astype(bf16)
        if part_ref is not None:
            pack(part_ref, 0, turn_ref, turn_ref.shape[0], 1, cols)


def layer_backward(pair, slope, down, up, d_h2, unit, scaled, gain1, out_weight, ctx, vec, cols, dealt):
    tokens, width = d_h2.shape
    units = up.shape[1]
    chunk = width
    square = (tokens, width)
    shapes = [(square, f32), ((tokens + EXTRA, width), bf16), ((tokens, units), bf16)]
    specs = [full(square), full((tokens + EXTRA, width)), step_cols(tokens, chunk)]
    kernel = functools.partial(layer_backward_kernel, cols)
    if dealt:
        shapes.append(((cols, units // cols, tokens), bf16))
        specs.append(full(shapes[-1][0]))
    else:
        kernel = lambda *refs: layer_backward_kernel(cols, *refs[:-2], None, *refs[-2:])
    return pl.pallas_call(
        kernel,
        grid=(units // chunk,),
        in_specs=[full((tokens, 2 * width)), step_cols(tokens, chunk), step_rows(chunk, width), step_cols(width, chunk),
                  full(square), full(square), full((tokens, PAIR)), full((1, width)), full(out_weight.shape), full(ctx.shape),
                  full((8, width))],
        out_specs=specs,
        out_shape=[jax.ShapeDtypeStruct(*x) for x in shapes],
        scratch_shapes=[pltpu.VMEM(square, f32), pltpu.VMEM((units, tokens), f32)],
        compiler_params=params(),
        cost_estimate=cost(1),
        name="layer_backward",
    )(pair, slope, down, up, d_h2, unit, scaled, gain1.reshape(1, width), out_weight, ctx, vec)


def layer_sums_kernel(rows, chunk, place_ref, pair_even_ref, pair_odd_ref, mine_ref, twin_ref, even_ref, odd_ref, act_ref,
                      din_ref, earlier_ref, *out_refs):
    *out_refs, out_ref = out_refs
    me = 2 * place_ref[0] + place_ref[1]
    width = mine_ref.shape[1]
    features = act_ref.shape[1] - chunk
    half = width // 2
    down = up = out = small = 0.0
    for i in range(act_ref.shape[0] // 2):
        part = lanes([act_ref[me ^ (2 * i)], act_ref[me ^ (2 * i + 1)]])
        din = lanes([din_ref[me ^ (2 * i)], din_ref[me ^ (2 * i + 1)]])
        normed = jnp.concatenate([pair_even_ref[i, :, :width], pair_odd_ref[i, :, :width]], axis=0)
        branch = jnp.concatenate([pair_even_ref[i, :, width:], pair_odd_ref[i, :, width:]], axis=0)
        first, second = (even_ref.at[i - 1], odd_ref.at[i - 1]) if i else (mine_ref, twin_ref)
        attn = jnp.concatenate([first[:TOK, :], second[:TOK, :]], axis=0)
        down = down + dot(part[:chunk], branch, NN)
        out = out + dot(part[chunk:], attn, NN)
        up = up + dot(din, normed, NN)
        small = small + first[TOK:, :].astype(f32) + second[TOK:, :].astype(f32)
    up = up.T
    small = small[EXTRA - 4:]
    share, size, few = width // rows, chunk // rows, features // rows
    for r in range(rows):
        vectors = lanes([small[:, r * share:(r + 1) * share], jnp.zeros((4, chunk - share), f32)])
        pieces = [
            down[r * size:(r + 1) * size, :half], down[r * size:(r + 1) * size, half:],
            up[r * share:(r + 1) * share],
            out[r * few:(r + 1) * few, :half], out[r * few:(r + 1) * few, half:],
            vectors, jnp.zeros((EXTRA - 4, chunk), f32),
        ]
        out_ref[r] = jnp.concatenate(pieces, axis=0).astype(bf16)
    for k, ref in enumerate(out_refs):
        ref[...] = out_ref[place_ref[2] ^ k]


def layer_sums(place, pair, attn, act, din, earlier, rows, chunk):
    width = attn[0].shape[1]
    features = act.shape[1] - chunk
    height = (2 * chunk + 2 * features) // rows + width // rows + EXTRA
    return pl.pallas_call(
        functools.partial(layer_sums_kernel, rows, chunk),
        in_specs=[scalar()] + [whole()] * 8 + [unread()],
        out_specs=[whole()] * rows,
        out_shape=[jax.ShapeDtypeStruct((height, chunk), bf16)] * rows,
        scratch_shapes=[pltpu.VMEM((rows, height, chunk), bf16)],
        compiler_params=params(),
        cost_estimate=cost(6),
        name="layer_sums",
    )(place, *pair, *attn, act, din, earlier)


def layer_unpack_kernel(cols, place_ref, even_ref, odd_ref, down_ref, up_ref, out_ref, small_ref):
    me = 2 * place_ref[0] + place_ref[1]
    half = down_ref.shape[1] // 2
    size, share, few = down_ref.shape[0] // cols, up_ref.shape[0], out_ref.shape[0] // cols
    chunk = up_ref.shape[1] // cols
    for ref, odd in ((even_ref, 0), (odd_ref, 1)):
        for i in range(cols // 2):
            spot = me ^ (2 * i + odd)
            part = ref[i].astype(f32)
            down_rows = pl.ds(pl.multiple_of(spot * size, 8), size)
            down_ref[down_rows, :half] = part[:size]
            down_ref[down_rows, half:] = part[size:2 * size]
            at = 2 * size + share
            up_ref[:, pl.ds(pl.multiple_of(spot * chunk, PAIR), chunk)] = part[2 * size:at]
            out_rows = pl.ds(pl.multiple_of(spot * few, 8), few)
            out_ref[out_rows, :half] = part[at:at + few]
            out_ref[out_rows, half:] = part[at + few:at + 2 * few]
            if i == 0 and not odd:
                small_ref[...] = part[at + 2 * few:at + 2 * few + 8, :share]


def layer_unpack(place, even, odd, rows, width, units):
    cols = 2 * even.shape[0]
    share = width // rows
    shapes = [(units // rows, width), (share, units), (share, width), (8, share)]
    return pl.pallas_call(
        functools.partial(layer_unpack_kernel, cols),
        in_specs=[scalar()] + [whole()] * 2,
        out_specs=[whole()] * 4,
        out_shape=[jax.ShapeDtypeStruct(x, f32) for x in shapes],
        compiler_params=params(),
        cost_estimate=cost(4),
        name="layer_unpack",
    )(place, even, odd)


def attn_sums_kernel(rows, place_ref, rows_ref, rel_ref, *refs):
    *out_refs, out_ref = refs[-rows - 1:]
    refs = refs[:-rows - 2]
    count = len(refs) // 2
    size = refs[0].shape[0]
    width, places = rows_ref.shape[1], rel_ref.shape[0]
    table_q = table_k = query = key = value = 0.0
    for j in range(count):
        rows_in = rows_ref[j * BLK:(j + 1) * BLK, :]
        q_ref, k_ref = refs[j], refs[count + j]
        query = query + dot(q_ref[:, places:], rows_in, NN)
        key = key + dot(k_ref[:, places:places + BLK], rows_in, NN)
        value = value + dot(k_ref[:, places + BLK:], rows_in, NN)
        table_k = table_k + q_ref[:, :places].astype(f32)
        table_q = table_q + k_ref[:, :places].astype(f32)
    query = query + dot(table_q.astype(bf16), rel_ref[...], NN)
    key = key + dot(table_k.astype(bf16), rel_ref[...], NN)
    pieces = [query, key, value]
    fill = -3 * size % PAIR
    if fill:
        pieces.append(jnp.zeros((fill, width), f32))
    full_sum = jnp.concatenate(pieces, axis=0).T
    share, spots = width // rows, places // rows
    wide = full_sum.shape[1]
    both = jnp.concatenate([table_q, table_k], axis=0)
    lines = 2 * size * spots // wide
    for r in range(rows):
        cut = both[:, r * spots:(r + 1) * spots]
        cut = lanes([cut[j * lines:(j + 1) * lines] for j in range(wide // spots)])
        out_ref[r] = jnp.concatenate([full_sum[r * share:(r + 1) * share], cut], axis=0).astype(bf16)
    for k, ref in enumerate(out_refs):
        ref[...] = out_ref[place_ref[2] ^ k]


def attn_sums(place, rows_in, rel, q_parts, k_parts, earlier, rows):
    size = q_parts[0].shape[0]
    width, places = rows_in.shape[1], rel.shape[0]
    wide = 3 * size + (-3 * size % PAIR)
    height = width // rows + 2 * size * (places // rows) // wide
    return pl.pallas_call(
        functools.partial(attn_sums_kernel, rows),
        in_specs=[scalar()] + [whole()] * (2 + len(q_parts) + len(k_parts)) + [unread()],
        out_specs=[whole()] * rows,
        out_shape=[jax.ShapeDtypeStruct((height, wide), bf16)] * rows,
        scratch_shapes=[pltpu.VMEM((rows, height, wide), bf16)],
        compiler_params=params(),
        cost_estimate=cost(5),
        name="attn_sums",
    )(place, rows_in, rel, *q_parts, *k_parts, earlier)


def rel_kernel(cols, share, spots, place_ref, even_ref, odd_ref, wq_ref, wk_ref, rel_ref, tq_ref, tk_ref):
    me = 2 * place_ref[0] + place_ref[1]
    width = wq_ref.shape[0]
    size = width // cols
    for ref, odd in ((even_ref, 0), (odd_ref, 1)):
        for i in range(cols // 2):
            spot = me ^ (2 * i + odd)
            tail = ref[i, share:, :].astype(f32)
            tail = jnp.concatenate([tail[:, j * spots:(j + 1) * spots] for j in range(tail.shape[1] // spots)], axis=0)
            at = pl.ds(pl.multiple_of((spot % 2) * (width // 2) + (spot // 2) * size, EXTRA), size)
            tq_ref[at, :] = tail[:size].astype(bf16)
            tk_ref[at, :] = tail[size:].astype(bf16)
    flip = flip_matrix(spots)
    across = (((0,), (1,)), ((), ()))
    turned_q = dot(tq_ref[...], flip, NN).astype(bf16)
    turned_k = dot(tk_ref[...], flip, NN).astype(bf16)
    rel_ref[...] = (dot(turned_q, wq_ref[...], across) + dot(turned_k, wk_ref[...], across)).astype(bf16)


def rel_share(place, even, odd, wq, wk, rows, places):
    cols = 2 * even.shape[0]
    width = wq.shape[0]
    spots = places // rows
    return pl.pallas_call(
        functools.partial(rel_kernel, cols, width // rows, spots),
        in_specs=[scalar()] + [whole()] * 4,
        out_specs=whole(),
        out_shape=jax.ShapeDtypeStruct((spots, width), bf16),
        scratch_shapes=[pltpu.VMEM((width, spots), bf16)] * 2,
        compiler_params=params(),
        cost_estimate=cost(2),
        name="rel_share",
    )(place, even, odd, wq, wk)


def attn_unpack_kernel(cols, place_ref, even_ref, odd_ref, earlier_ref, q_ref, k_ref, v_ref, all_ref):
    me = 2 * place_ref[0] + place_ref[1]
    share, width = q_ref.shape
    size = width // cols
    for ref, odd in ((even_ref, 0), (odd_ref, 1)):
        for i in range(cols // 2):
            all_ref[me ^ (2 * i + odd)] = ref[i, :share, :].astype(f32)
    for c in range(cols):
        start = (c % 2) * width // 2 + (c // 2) * size
        for i, ref in enumerate((q_ref, k_ref, v_ref)):
            ref[:, start:start + size] = all_ref[c, :, i * size:(i + 1) * size]


def attn_unpack(place, even, odd, earlier, rows, width):
    count, _, wide = even.shape
    share = width // rows
    return pl.pallas_call(
        functools.partial(attn_unpack_kernel, 2 * count),
        in_specs=[scalar()] + [whole()] * 2 + [unread()],
        out_specs=[whole()] * 3,
        out_shape=[jax.ShapeDtypeStruct((share, width), f32)] * 3,
        scratch_shapes=[pltpu.VMEM((2 * count, share, wide), f32)],
        compiler_params=params(),
        cost_estimate=cost(4),
        name="attn_unpack",
    )(place, even, odd, earlier)


HEADS = 12


def mul(a, b, form=NN):
    return lax.dot_general(a, b, form, preferred_element_type=f32)


def swap(x, axis, k):
    return lax.ppermute(x, axis, [(i, i ^ k) for i in range(lax.axis_size(axis))])


def gather(x, *earlier):
    even = stack([x] + [swap(x, "seq", k) for k in range(2, lax.axis_size("seq"), 2)], *earlier)
    return even, swap(even, "seq", 1)


def gather_parts(x, *earlier):
    twin = swap(x, "seq", 1)
    even = stack([swap(x, "seq", k) for k in range(2, lax.axis_size("seq"), 2)], *earlier)
    return x, twin, even, swap(even, "seq", 1)


def deal_rows(parts, *earlier):
    return sum_arrays([swap(part, "row", k) if k else part for k, part in enumerate(parts)], *earlier)


def deal_chips(parts):
    return [parts[0]] + [swap(part, "seq", 2 * k) for k, part in enumerate(parts) if k]


def in_order(parts, chip):
    out = jnp.zeros((len(parts),) + parts[0].shape, parts[0].dtype)
    for k, part in enumerate(parts):
        out = lax.dynamic_update_slice_in_dim(out, part[None], chip ^ k, 0)
    return out.reshape((-1,) + parts[0].shape[1:])


def reduced(g):
    part = lax.psum_scatter(g.astype(bf16), "row", scatter_dimension=0, tiled=True)
    return lax.psum(part, "seq").astype(f32)


def on_device(
    hidden, segments, rel_embed, query_weight, key_weight, value_weight, output_weight, up_weight, down_weight,
    norm1_gain, norm1_bias, norm2_gain, norm2_bias, cotangent,
):
    tokens, width = hidden.shape[1:]
    places = rel_embed.shape[0]
    units = up_weight.shape[1]
    part = width // 2
    scale = 1.0 / math.sqrt(3.0 * (width // HEADS))
    inputs = hidden[0]
    cols, rows = lax.axis_size("seq"), lax.axis_size("row")
    chip, core = lax.axis_index("seq") // 2, lax.axis_index("seq") % 2
    row = lax.axis_index("row")
    place = jnp.stack([chip, core, row]).astype(jnp.int32)
    share = width // rows
    chunk = units // cols
    dealt = (units // (rows * cols)) % 16 == 0 and places // rows == TOK

    def core_cols(w):
        return lax.dynamic_slice_in_dim(w, core * part, part, 1)

    def meet(x):
        mine = lax.dynamic_index_in_dim(x, core, 0, keepdims=False)
        other = swap(lax.dynamic_index_in_dim(x, 1 - core, 0, keepdims=False), "seq", 1)
        return jnp.where(core == 0, jnp.concatenate([mine, other], axis=-1), jnp.concatenate([other, mine], axis=-1))

    half_q, half_k, half_v = core_cols(query_weight), core_cols(key_weight), core_cols(value_weight)
    half_out = lax.dynamic_slice_in_dim(output_weight, core * part, part, 0)
    rel_flip = mul(flip_matrix(places), rel_embed).astype(bf16)
    qr = mul(rel_flip, half_q).astype(bf16)
    kr = mul(rel_flip, half_k).astype(bf16)
    seg_rows = jnp.pad(segments.astype(bf16), ((0, EXTRA - 1), (0, width - tokens)))
    in_parts = gather_parts(jnp.concatenate([inputs, seg_rows], axis=0), qr, kr)
    q, k, v, row_segs, row_in = project_rows(place, in_parts, half_q, half_k, half_v)
    own_segs = row_segs[0, :BLK].reshape(BLK, 1)

    probs, ctx_half = forward_attention(place, q, k, v, kr, qr, own_segs, row_segs, scale)
    ctx = meet(ctx_half)

    norms = (norm1_gain, norm1_bias, norm2_gain, norm2_bias)
    output, pair_low, active_low, slope, unit1, scaled1, d_h2, vec, *act = layer_forward(
        inputs, ctx, output_weight, up_weight, down_weight, cotangent[0], norms, cols, rows, dealt
    )
    d_h1, attn_pay, d_inner, *parts = layer_backward(
        pair_low, slope, down_weight, up_weight, d_h2, unit1, scaled1, norm1_gain, output_weight, ctx, vec, cols, dealt
    )
    if dealt:
        act, = (lax.all_to_all(x, "seq", 0, 0, tiled=True) for x in act)

        parts, = parts
        pair = gather(pair_low, attn_pay)
        parts = lax.all_to_all(after(parts, act), "seq", 0, 0, tiled=True)
    else:
        act = parts = attn_pay
    twin = swap(attn_pay, "seq", 1)
    dq_half, *q_table = query_grads(place, probs, attn_pay, twin, half_out, ctx_half, v, q, k, kr, attn_pay, scale)
    even = stack([swap(attn_pay, "seq", i) for i in range(2, cols, 2)], dq_half)
    attn = attn_pay, twin, even, swap(even, "seq", 1)
    if dealt:
        layer_part = layer_sums(place, pair, attn, act, parts, dq_half, rows, chunk)
    dk_half, dv_half, *k_table = key_grads(
        place, k, v, q, qr, kr, own_segs, row_segs, attn, half_out, layer_part[0] if dealt else act, scale
    )
    d_own = meet(jnp.concatenate([dq_half, dk_half, dv_half], axis=1))
    dq, dk, dv = (d_own[i * tokens:(i + 1) * tokens] for i in range(3))
    grad_in = d_h1 + mul(dq, query_weight, NT) + mul(dk, key_weight, NT) + mul(dv, value_weight, NT)
    grad_in = grad_in.astype(bf16)

    if dealt:
        k_parts = deal_chips(k_table)
        layer = deal_rows(layer_part, dk_half)
        q_parts = deal_chips(q_table)
        attn_part = attn_sums(place, row_in, rel_flip, q_parts, k_parts, layer, rows)
        attn_sum = deal_rows(attn_part)
        g_down, g_up, g_output, small = layer_unpack(place, *gather(after(layer, attn_part[0]), attn_sum), rows, width, units)
        sums = gather(attn_sum)
        g_rel = rel_share(place, *sums, query_weight, key_weight, rows, places)
        g_query, g_key, g_value = attn_unpack(place, *sums, g_rel, rows, width)
        g_rel = join_rows(place, [g_rel] + [swap(g_rel, "row", k) for k in range(1, rows)], small, grad_in)
    else:
        small = jnp.stack([reduced(x) for x in attn_pay[tokens + EXTRA - 4:]])
        g_down = reduced(mul(active_low, pair_low[:, width:], TN))
        g_up = reduced(mul(pair_low[:, :width], d_inner, TN))
        g_output = reduced(mul(ctx[:tokens].astype(bf16), attn_pay[:tokens], TN))
        across = (((0,), (1,)), ((), ()))
        d_kr, d_qr = (in_order(x, chip)[:, :places] for x in (q_table, k_table))
        placed = lambda g: lax.dynamic_update_slice_in_dim(jnp.zeros((width, width), f32), g, core * part, 1)
        g_query = reduced(mul(inputs, dq, TN) + placed(mul(rel_flip, d_qr, across)))
        g_key = reduced(mul(inputs, dk, TN) + placed(mul(rel_flip, d_kr, across)))
        g_value = reduced(mul(inputs, dv, TN))
        g_rel = mul(d_qr, half_q, across) + mul(d_kr, half_k, across)
        g_rel = lax.psum(mul(flip_matrix(places), g_rel.astype(bf16)).astype(bf16), ("seq", "row")).astype(f32)

    return (
        output[None], grad_in[None], g_query, g_key, g_value, g_output, g_up, g_down,
        small[0], small[1], small[2], small[3], g_rel,
    )


def solution(mesh):
    split = P("row", "seq", None)
    return jax.shard_map(
        on_device,
        mesh=mesh,
        in_specs=(split, P("row", "seq")) + (P(),) * 11 + (split,),
        out_specs=(split, split) + (P("row", None),) * 6 + (P("row"),) * 4 + (P(),),
        check_vma=False,
    )
```

```python
import functools, math
import jax, jax.numpy as jnp
from jax import lax
from jax.experimental import pallas as pl
from jax.experimental.pallas import tpu as pltpu
from jax.sharding import PartitionSpec as P

BLK = 256
TOK = 128
PAIR = 128
EXTRA = 16
COST = 1e6
EPSILON = 1e-07
NT = (((1,), (1,)), ((), ()))
NN = (((1,), (0,)), ((), ()))
TN = (((0,), (0,)), ((), ()))
bf16 = jnp.bfloat16
f32 = jnp.float32


def dot(a, b, form):
    return lax.dot_general(a, b, form, preferred_element_type=f32)


def lanes(parts):
    return jnp.concatenate(parts, axis=1)


def half_masks(x):
    lane = lax.broadcasted_iota(jnp.int32, x.shape, 1)
    low = lane < PAIR // 2
    zero = jnp.zeros_like(x)
    return jnp.where(low, x, zero), jnp.where(low, zero, x)


def join_heads(stacked, rows):
    lane = lax.broadcasted_iota(jnp.int32, (rows, PAIR), 1)
    return jnp.where(lane < PAIR // 2, stacked[:rows], stacked[rows:])


def block_start(chip, slot):
    return pl.multiple_of((chip ^ slot) * BLK, BLK)


def fill_table(out_ref, flip_ref, start):
    places = flip_ref.shape[0]
    low = jnp.broadcast_to(flip_ref[0:1, :], (BLK, PAIR))
    high = jnp.broadcast_to(flip_ref[places - 1:places, :], (BLK, PAIR))
    for b in range(out_ref.shape[0] // BLK):
        out_ref[b * BLK:(b + 1) * BLK, :] = jnp.where(b * BLK < start, low, high)
    out_ref[pl.ds(pl.multiple_of(start, BLK), places), :] = flip_ref[...]


def fill_scores(chip, own_ref, all_ref, near_ref, far_ref, s_ref, n_ref, length):
    wide = length + BLK
    own = jnp.concatenate(half_masks(own_ref[...]), axis=0)
    ext = dot(own, near_ref[...], NT)
    for h in range(2):
        moved = pltpu.roll(ext[h * BLK:(h + 1) * BLK], wide - (BLK - 1), 1, stride=1, stride_axis=0)
        n_ref[h] = moved[:, :length]
    for slot in range(length // BLK):
        cols = slice(slot * BLK, (slot + 1) * BLK)
        blk = all_ref[cols, :]
        both = jnp.concatenate(half_masks(blk), axis=0)
        start = block_start(chip, slot)
        win = far_ref[pl.ds(pl.multiple_of(length - BLK - start, BLK), 2 * BLK), :]
        back = dot(both, win, NT)
        direct = dot(own, blk, NT)
        for h in range(2):
            rows = slice(h * BLK, (h + 1) * BLK)
            moved = pltpu.roll(back[rows], BLK + 1, 1, stride=1, stride_axis=0)[:, :BLK]
            s_ref[h, :, cols] = direct[rows] + moved.T + n_ref[h, :, pl.ds(start, BLK)]


def far_start(chip, length):
    return length - BLK - chip * BLK


def forward_kernel(scale, length, place_ref, q_ref, k_ref, v_ref, near_ref, far_ref, segq_ref, segk_ref,
                   p_ref, out_ref, s_ref, n_ref, near_tab, far_tab):
    chip = place_ref[0]
    fill_table(near_tab, near_ref, chip * BLK)
    fill_table(far_tab, far_ref, far_start(chip, length))
    fill_scores(chip, q_ref, k_ref, near_tab, far_tab, s_ref, n_ref, length)
    allowed = segq_ref[...] == segk_ref[...]
    stats = []
    for h in range(2):
        logits = jnp.where(allowed, s_ref[h] * scale, -1e30)
        best = jnp.max(logits, axis=1, keepdims=True)
        weights = jnp.exp(logits - best)
        total = jnp.sum(weights, axis=1, keepdims=True)
        p_ref[h] = (weights * (1.0 / total)).astype(bf16)
        stats.append(best + jnp.log(total))
    stacked = jnp.concatenate([p_ref[0], p_ref[1]], axis=0)
    ctx = join_heads(dot(stacked, v_ref[...], NN), BLK)
    lane = lax.broadcasted_iota(jnp.int32, (TOK, PAIR), 1)
    for c in range(2):
        rows = slice(c * TOK, (c + 1) * TOK)
        out_ref[c, :TOK, :] = ctx[rows]
        out_ref[c, TOK:, :] = jnp.where(lane == 0, stats[0][rows], stats[1][rows]).T[:8]


def flip_matrix(count):
    r = lax.broadcasted_iota(jnp.int32, (count, count), 0)
    c = lax.broadcasted_iota(jnp.int32, (count, count), 1)
    return jnp.where(r + c == count - 1, 1.0, 0.0).astype(bf16)


def fold_table(grad, start, places, fold_ref):
    place = lax.broadcasted_iota(jnp.int32, grad.shape, 1)
    low = jnp.sum(jnp.where(place < start, grad, 0.0), axis=1, keepdims=True)
    high = jnp.sum(jnp.where(place >= start + places, grad, 0.0), axis=1, keepdims=True)
    fold_ref[...] = grad
    table = fold_ref[:, pl.ds(pl.multiple_of(start, BLK), places)]
    spot = lax.broadcasted_iota(jnp.int32, table.shape, 1)
    return table + jnp.where(spot == 0, low, 0.0) + jnp.where(spot == places - 1, high, 0.0)


def grads_tail(scale, length, places, chip, ds_ref, own_ref, all_ref, near_ref, table_ref, wide_ref, down_ref, fold_ref, n_ref):
    flip = flip_matrix(BLK)
    rows = pair_rows()
    for h in range(2):
        back = dot(flip, ds_ref[h], NN)
        down_ref[h * BLK:(h + 1) * BLK, :] = back.astype(bf16)
        for slot in range(length // BLK):
            n_ref[h, :, pl.ds(block_start(chip, slot), BLK)] = back[:, slot * BLK:(slot + 1) * BLK]
        padded = lanes([n_ref[h], jnp.zeros((BLK, BLK), f32)])
        wide_ref[h * BLK:(h + 1) * BLK, :] = pltpu.roll(padded, 0, 1, stride=1, stride_axis=0).astype(bf16)
    own_grad = dot(down_ref[...], all_ref[...], NN) + dot(wide_ref[...], near_ref[...], NN)
    own_grad = (join_heads(own_grad, BLK) * scale).astype(bf16)
    table_ref[rows, places:places + BLK] = dot(own_grad, flip, TN).astype(bf16)
    own_grad = dot(flip, own_grad, NN).astype(bf16)
    own = dot(flip, own_ref[...], NN).astype(bf16)
    own = jnp.concatenate(half_masks(own), axis=0)
    near_grad = dot(own, wide_ref[...], TN) * scale
    table_ref[rows, :places] = fold_table(near_grad, chip * BLK, places, fold_ref).astype(bf16)
    return own_grad


def pair_rows():
    return pl.ds(pl.multiple_of(pl.program_id(0) * PAIR, PAIR), PAIR)


def deal_table(chip, table_ref, out_refs):
    @pl.when(pl.program_id(0) == pl.num_programs(0) - 1)
    def _():
        for k, ref in enumerate(out_refs):
            size = ref.shape[0]
            ref[...] = table_ref[pl.ds(pl.multiple_of((chip ^ k) * size, EXTRA), size), :]


def split_tokens(out_ref, value):
    for c in range(2):
        out_ref[c] = value[c * TOK:(c + 1) * TOK]


def query_grad_kernel(scale, length, chips, place_ref, p_ref, mine_ref, twin_ref, out_weight_ref, ctx_ref, v_ref, q_ref, k_ref,
                      near_ref, earlier_ref, dq_ref, *refs):
    out_refs, (near_tab, dctx_ref, table_ref, ds_ref, *scratch) = refs[:chips], refs[chips:]
    chip, core = place_ref[0], place_ref[1]
    places = near_ref.shape[0]
    fill_table(near_tab, near_ref, chip * BLK)
    for ref, at in ((mine_ref, core), (twin_ref, 1 - core)):
        rows = pl.ds(pl.multiple_of(at * TOK, TOK), TOK)
        dctx_ref[rows, :] = dot(ref[:TOK, :], out_weight_ref[...], NT).astype(bf16)
    dctx = jnp.concatenate(half_masks(dctx_ref[...]), axis=0)
    dprob = dot(dctx, v_ref[...], NT)
    ctx = jnp.concatenate([ctx_ref[0, :TOK, :], ctx_ref[1, :TOK, :]], axis=0)
    for h in range(2):
        rows = slice(h * BLK, (h + 1) * BLK)
        row_dot = jnp.sum(dctx[rows].astype(f32) * ctx, axis=1, keepdims=True)
        ds_ref[h] = (p_ref[h].astype(f32) * (dprob[rows] - row_dot)).astype(bf16)
    dq = grads_tail(scale, length, places, chip, ds_ref, q_ref, k_ref, near_tab, table_ref, *scratch)
    split_tokens(dq_ref, dq)
    deal_table(chip, table_ref, out_refs)


def key_grad_kernel(scale, length, pairs, chips, place_ref, k_ref, v_ref, q_ref, near_ref, far_ref, segk_ref, segq_ref,
                    mine_ref, twin_ref, even_ref, odd_ref, out_weight_ref, earlier_ref, dk_ref, dv_ref, *refs):
    out_refs, refs = refs[:chips], refs[chips:]
    s_ref, near_tab, far_tab, dctx_ref, p_ref, stat_ref, table_ref, ds_ref, *scratch = refs
    chip, core = place_ref[0], place_ref[1]
    places = near_ref.shape[0]
    fill_table(near_tab, near_ref, chip * BLK)
    fill_table(far_tab, far_ref, far_start(chip, length))
    fill_scores(chip, k_ref, q_ref, near_tab, far_tab, s_ref, scratch[-1], length)
    stat_cols = pl.ds(pl.multiple_of((core * pairs + pl.program_id(0)) * PAIR, PAIR), PAIR)
    for slot in range(length // BLK):
        for odd in range(2):
            at = pl.ds(pl.multiple_of(slot * BLK + (core ^ odd) * TOK, TOK), TOK)
            if slot == 0:
                ref = twin_ref if odd else mine_ref
            else:
                ref = (odd_ref if odd else even_ref).at[slot - 1]
            dctx_ref[at, :] = dot(ref[:TOK, :], out_weight_ref[...], NT).astype(bf16)
            stat_ref[:, at] = ref[TOK:, stat_cols].astype(f32)
    merged = [stat_ref[3 * j:3 * j + 1] + stat_ref[3 * j + 1:3 * j + 2] + stat_ref[3 * j + 2:3 * j + 3] for j in range(4)]
    allowed = segk_ref[...] == segq_ref[...]
    dctx = dctx_ref[...]
    vals = jnp.concatenate(half_masks(v_ref[...]), axis=0)
    dprob = dot(vals, dctx, NT)
    for h in range(2):
        rows = slice(h * BLK, (h + 1) * BLK)
        probs = jnp.where(allowed, jnp.exp(s_ref[h] * scale - merged[h]), 0.0)
        p_ref[rows, :] = probs.astype(bf16)
        ds_ref[h] = (probs * (dprob[rows] - merged[2 + h])).astype(bf16)
    dv = join_heads(dot(p_ref[...], dctx, NN), BLK)
    split_tokens(dv_ref, dv.astype(bf16))
    table_ref[pair_rows(), places + BLK:] = dv.T.astype(bf16)
    dk = grads_tail(scale, length, places, chip, ds_ref, k_ref, q_ref, near_tab, table_ref, *scratch)
    split_tokens(dk_ref, dk)
    deal_table(chip, table_ref, out_refs)


def col(rows):
    return pl.BlockSpec((rows, PAIR), lambda p: (0, p))


def full(shape):
    return pl.BlockSpec(shape, lambda p: (0,) * len(shape))


def whole():
    return pl.BlockSpec(memory_space=pltpu.VMEM)


def scalar():
    return pl.BlockSpec(memory_space=pltpu.SMEM)


def unread():
    return pl.BlockSpec(memory_space=pl.ANY)


def params():
    return pltpu.CompilerParams(vmem_limit_bytes=56 * 1024 * 1024)


def cost(microseconds):
    return pl.CostEstimate(flops=int(microseconds * COST), bytes_accessed=0, transcendentals=0)


def after(x, *earlier):
    def kernel(*refs):
        pass

    return pl.pallas_call(
        kernel,
        in_specs=[unread()] * (1 + len(earlier)),
        out_specs=unread(),
        out_shape=jax.ShapeDtypeStruct(x.shape, x.dtype),
        input_output_aliases={0: 0},
        cost_estimate=cost(0.1),
        name="after",
    )(x, *earlier)


def stack_kernel(count, *refs):
    for i in range(count):
        refs[-1][i] = refs[i][...]


def stack(arrays, *earlier):
    count = len(arrays)
    return pl.pallas_call(
        functools.partial(stack_kernel, count),
        in_specs=[whole()] * count + [unread()] * len(earlier),
        out_specs=whole(),
        out_shape=jax.ShapeDtypeStruct((count,) + arrays[0].shape, arrays[0].dtype),
        compiler_params=params(),
        cost_estimate=cost(1),
        name="stack",
    )(*arrays, *earlier)


def sum_kernel(count, *refs):
    total = 0.0
    for ref in refs[:count]:
        total = total + ref[...].astype(f32)
    refs[-1][...] = total.astype(bf16)


def sum_arrays(arrays, *earlier):
    count = len(arrays)
    return pl.pallas_call(
        functools.partial(sum_kernel, count),
        in_specs=[whole()] * count + [unread()] * len(earlier),
        out_specs=whole(),
        out_shape=jax.ShapeDtypeStruct(arrays[0].shape, bf16),
        compiler_params=params(),
        cost_estimate=cost(1),
        name="sum_rows",
    )(*arrays, *earlier)


def join_kernel(place_ref, *refs):
    *refs, _, _, out_ref = refs
    size = refs[0].shape[0]
    for k, ref in enumerate(refs):
        spot = len(refs) - 1 - (place_ref[2] ^ k)
        out_ref[pl.ds(pl.multiple_of(spot * size, size), size), :] = ref[...].astype(f32)


def join_rows(place, blocks, *earlier):
    size, width = blocks[0].shape
    return pl.pallas_call(
        join_kernel,
        in_specs=[scalar()] + [whole()] * len(blocks) + [unread()] * 2,
        out_specs=whole(),
        out_shape=jax.ShapeDtypeStruct((len(blocks) * size, width), f32),
        compiler_params=params(),
        cost_estimate=cost(1),
        name="join_rows",
    )(place, *blocks, *earlier)


def table_scratch(length):
    return pltpu.VMEM((length + BLK, PAIR), bf16)


def probs_block(length):
    return pl.BlockSpec((2, BLK, length), lambda p: (p, 0, 0))


def token_block():
    return pl.BlockSpec((2, TOK, PAIR), lambda p: (0, 0, p))


def forward_attention(place, q, k, v, near, far, seg_q, seg_k, scale):
    length, width = k.shape
    places = near.shape[0]
    pairs = width // PAIR
    return pl.pallas_call(
        functools.partial(forward_kernel, scale, length),
        grid=(pairs,),
        in_specs=[scalar(), col(BLK), col(length), col(length), col(places), col(places), full((BLK, 1)), full((1, length))],
        out_specs=[probs_block(length), pl.BlockSpec((2, TOK + 8, PAIR), lambda p: (0, 0, p))],
        out_shape=[
            jax.ShapeDtypeStruct((2 * pairs, BLK, length), bf16),
            jax.ShapeDtypeStruct((2, TOK + 8, width), f32),
        ],
        scratch_shapes=[pltpu.VMEM((2, BLK, length), f32)] * 2 + [table_scratch(length)] * 2,
        compiler_params=params(),
        cost_estimate=cost(14),
        name="attend",
    )(place, q, k, v, near, far, seg_q, seg_k)


def grad_scratch(length):
    return [
        pltpu.VMEM((2, BLK, length), bf16),
        pltpu.VMEM((2 * BLK, length + BLK), bf16),
        pltpu.VMEM((2 * BLK, length), bf16),
        pltpu.VMEM((PAIR, length + BLK), f32),
        pltpu.VMEM((2, BLK, length), f32),
    ]


def query_grads(place, p, mine, twin, out_weight, ctx, v, q, k, near, earlier, scale):
    length, width = k.shape
    places = near.shape[0]
    chips = length // BLK
    table = jax.ShapeDtypeStruct((width // chips, places + BLK), bf16)
    return pl.pallas_call(
        functools.partial(query_grad_kernel, scale, length, chips),
        grid=(width // PAIR,),
        in_specs=[scalar(), probs_block(length), full(mine.shape), full(twin.shape),
                  pl.BlockSpec((PAIR, out_weight.shape[1]), lambda p: (p, 0)),
                  pl.BlockSpec((2, TOK + 8, PAIR), lambda p: (0, 0, p)), col(length), col(BLK), col(length), col(places),
                  unread()],
        out_specs=[token_block()] + [full(table.shape)] * chips,
        out_shape=[jax.ShapeDtypeStruct((2, TOK, width), bf16)] + [table] * chips,
        scratch_shapes=[table_scratch(length), pltpu.VMEM((BLK, PAIR), bf16), pltpu.VMEM((width, places + BLK), bf16)]
        + grad_scratch(length),
        compiler_params=params(),
        cost_estimate=cost(1),
        name="query_grads",
    )(place, p, mine, twin, out_weight, ctx, v, q, k, near, earlier)


def key_grads(place, k, v, q, near, far, seg_k, seg_q, attn, out_weight, earlier, scale):
    length, width = q.shape
    places = near.shape[0]
    pairs = width // PAIR
    chips = length // BLK
    table = jax.ShapeDtypeStruct((width // chips, places + 2 * BLK), bf16)
    return pl.pallas_call(
        functools.partial(key_grad_kernel, scale, length, pairs, chips),
        grid=(pairs,),
        in_specs=[scalar(), col(BLK), col(BLK), col(length), col(places), col(places), full((BLK, 1)), full((1, length))]
        + [full(x.shape) for x in attn]
        + [pl.BlockSpec((PAIR, out_weight.shape[1]), lambda p: (p, 0)), unread()],
        out_specs=[token_block(), token_block()] + [full(table.shape)] * chips,
        out_shape=[jax.ShapeDtypeStruct((2, TOK, width), bf16)] * 2 + [table] * chips,
        scratch_shapes=[pltpu.VMEM((2, BLK, length), f32), table_scratch(length), table_scratch(length),
                        pltpu.VMEM((length, PAIR), bf16), pltpu.VMEM((2 * BLK, length), bf16),
                        pltpu.VMEM((EXTRA, length), f32), pltpu.VMEM((width, places + 2 * BLK), bf16)]
        + grad_scratch(length),
        compiler_params=params(),
        cost_estimate=cost(1),
        name="key_grads",
    )(place, k, v, q, near, far, seg_k, seg_q, *attn, out_weight, earlier)


def project_kernel(place_ref, mine_ref, twin_ref, even_ref, odd_ref, wq_ref, wk_ref, wv_ref, q_ref, k_ref, v_ref, seg_ref,
                   rows_ref):
    core = place_ref[1]
    count = even_ref.shape[0] + 1

    @pl.when(pl.program_id(0) == 0)
    def _():
        for slot in range(count):
            for odd in range(2):
                at = pl.ds(pl.multiple_of(slot * BLK + (core ^ odd) * TOK, TOK), TOK)
                if slot == 0:
                    ref = twin_ref if odd else mine_ref
                else:
                    ref = (odd_ref if odd else even_ref).at[slot - 1]
                rows_ref[at, :] = ref[:TOK, :]
                seg_ref[:, at] = ref[TOK:, :TOK].astype(f32)[:1]

    weights = lanes([wq_ref[...], wk_ref[...], wv_ref[...]])
    out = dot(rows_ref[...], weights, NN).astype(bf16)
    q_ref[...] = out[:, :PAIR]
    k_ref[...] = out[:, PAIR:2 * PAIR]
    v_ref[...] = out[:, 2 * PAIR:]


def project_rows(place, parts, wq, wk, wv):
    width, part = wq.shape
    length = BLK * (parts[2].shape[0] + 1)
    shape = jax.ShapeDtypeStruct((length, part), bf16)
    return pl.pallas_call(
        project_kernel,
        grid=(part // PAIR,),
        in_specs=[scalar()] + [full(x.shape) for x in parts] + [col(width)] * 3,
        out_specs=[col(length)] * 3 + [full((1, length)), full((length, width))],
        out_shape=[shape] * 3 + [jax.ShapeDtypeStruct((1, length), f32), jax.ShapeDtypeStruct((length, width), bf16)],
        compiler_params=params(),
        cost_estimate=cost(5),
        name="project",
    )(place, *parts, wq, wk, wv)


def mean(x):
    return jnp.mean(x, axis=-1, keepdims=True)


def norm_forward(value):
    center = value - mean(value)
    scaled = lax.rsqrt(mean(center * center) + EPSILON)
    return center * scaled, scaled


def norm_backward(grad_out, normed, scaled, gain):
    grad_normed = grad_out * gain
    inner = grad_normed - mean(grad_normed) - normed * mean(grad_normed * normed)
    return scaled * inner, jnp.sum(grad_out * normed, axis=0, keepdims=True), jnp.sum(grad_out, axis=0, keepdims=True)


def turn(turn_ref, at, value):
    for i in range(value.shape[1] // PAIR):
        turn_ref[pl.ds(pl.multiple_of(at + i * PAIR, PAIR), PAIR), :] = value[:, i * PAIR:(i + 1) * PAIR].T


def pack(out_ref, top, turn_ref, count, shares, cols):
    size = count // (shares * cols)
    for c in range(cols):
        starts = [r * (count // shares) + c * size for r in range(shares)]
        rows = jnp.concatenate([turn_ref[a:a + size, :] for a in starts], axis=0)
        out_ref[c, top:top + shares * size, :] = rows.astype(bf16)


def layer_forward_kernel(cols, rows, in_ref, ctx_ref, out_weight_ref, up_ref, down_ref, cot_ref, gain1_ref, bias1_ref,
                         gain2_ref, bias2_ref, output_ref, pair_ref, active_ref, slope_ref, unit_ref, scaled_ref,
                         d_h2_ref, vec_ref, part_ref, normed_ref, sum_ref, turn_ref):
    step = pl.program_id(0)
    tokens, width = in_ref.shape
    chunk = up_ref.shape[1]

    @pl.when(step == 0)
    def _():
        h1 = in_ref[...].astype(f32) + dot(ctx_ref[:tokens, :].astype(bf16), out_weight_ref[...], NN)
        unit, scaled = norm_forward(h1)
        unit_ref[...] = unit
        scaled_ref[...] = jnp.broadcast_to(scaled, scaled_ref.shape)
        normed = unit * gain1_ref[...] + bias1_ref[...]
        normed_ref[...] = normed.astype(bf16)
        pair_ref[:, :width] = normed.astype(bf16)
        sum_ref[...] = normed

    inner = dot(normed_ref[...], up_ref[...], NN)
    upper = 0.5 * (1.0 + lax.erf(inner * math.sqrt(0.5)))
    slope_ref[...] = upper + inner * jnp.exp(-0.5 * inner * inner) * (1.0 / math.sqrt(2.0 * math.pi))
    active = (inner * upper).astype(bf16)
    active_ref[...] = active
    sum_ref[...] += dot(active, down_ref[...], NN)
    if part_ref is not None:
        turn(turn_ref, step * chunk, active.astype(f32))

    @pl.when(step == pl.num_programs(0) - 1)
    def _():
        unit, scaled = norm_forward(sum_ref[...])
        output_ref[...] = (unit * gain2_ref[...] + bias2_ref[...]).astype(bf16)
        d_h2, g_gain, g_bias = norm_backward(cot_ref[...].astype(f32), unit, scaled, gain2_ref[...])
        d_h2_ref[...] = d_h2
        pair_ref[:, width:] = d_h2.astype(bf16)
        vec_ref[...] = jnp.concatenate([g_gain, g_bias] * 4, axis=0)
        if part_ref is not None:
            units = turn_ref.shape[0]
            pack(part_ref, 0, turn_ref, units, rows, cols)
            turn(turn_ref, 0, ctx_ref[:tokens, :])
            pack(part_ref, units // cols, turn_ref, width, rows, cols)


def step_cols(rows, chunk):
    return pl.BlockSpec((rows, chunk), lambda i: (0, i))


def step_rows(chunk, cols):
    return pl.BlockSpec((chunk, cols), lambda i: (i, 0))


def layer_forward(inputs, ctx, out_weight, up, down, cot, vectors, cols, rows, dealt):
    tokens, width = inputs.shape
    units = up.shape[1]
    chunk = width
    square = (tokens, width)
    shapes = [(square, bf16), ((tokens, 2 * width), bf16), ((tokens, units), bf16), ((tokens, units), f32), (square, f32),
              ((tokens, PAIR), f32), (square, f32), ((8, width), f32)]
    specs = [full(square), full((tokens, 2 * width)), step_cols(tokens, chunk), step_cols(tokens, chunk), full(square),
             full((tokens, PAIR)), full(square), full((8, width))]
    kernel = functools.partial(layer_forward_kernel, cols, rows)
    if dealt:
        shapes.append(((cols, (units + width) // cols, tokens), bf16))
        specs.append(full(shapes[-1][0]))
    else:
        kernel = lambda *refs: layer_forward_kernel(cols, rows, *refs[:-3], None, *refs[-3:])
    return pl.pallas_call(
        kernel,
        grid=(units // chunk,),
        in_specs=[full(square), full(ctx.shape), full(out_weight.shape), step_cols(width, chunk), step_rows(chunk, width),
                  full(square)] + [full((1, width))] * 4,
        out_specs=specs,
        out_shape=[jax.ShapeDtypeStruct(*x) for x in shapes],
        scratch_shapes=[pltpu.VMEM(square, bf16), pltpu.VMEM(square, f32), pltpu.VMEM((units, tokens), f32)],
        compiler_params=params(),
        cost_estimate=cost(1),
        name="layer_forward",
    )(inputs, ctx, out_weight, up, down, cot, *(x.reshape(1, width) for x in vectors))


def layer_backward_kernel(cols, pair_ref, slope_ref, down_ref, up_ref, d_h2_ref, unit_ref, scaled_ref, gain1_ref,
                          out_weight_ref, ctx_ref, vec_ref, d_h1_ref, pay_ref, din_ref, part_ref, sum_ref, turn_ref):
    step = pl.program_id(0)
    tokens, width = d_h2_ref.shape
    chunk = up_ref.shape[1]
    d_inner = (dot(pair_ref[:, width:], down_ref[...], NT) * slope_ref[...]).astype(bf16)
    din_ref[...] = d_inner
    part = dot(d_inner, up_ref[...], NT)
    if part_ref is not None:
        turn(turn_ref, step * chunk, d_inner.astype(f32))

    @pl.when(step == 0)
    def _():
        sum_ref[...] = d_h2_ref[...] + part

    @pl.when(step > 0)
    def _():
        sum_ref[...] += part

    @pl.when(step == pl.num_programs(0) - 1)
    def _():
        d_h1, g_gain, g_bias = norm_backward(sum_ref[...], unit_ref[...], scaled_ref[:, :1], gain1_ref[...])
        d_h1_ref[...] = d_h1
        d_attn = d_h1.astype(bf16)
        pay_ref[:tokens, :] = d_attn
        vectors = jnp.concatenate([g_gain, g_bias, vec_ref[:2]], axis=0)
        half = PAIR // 2
        for p in range(width // PAIR):
            at = slice(p * PAIR, (p + 1) * PAIR)
            d_ctx = dot(d_attn, out_weight_ref[at, :], NT).astype(bf16)
            turned = (d_ctx.astype(f32) * ctx_ref[:tokens, at]).T
            rows = [ctx_ref[tokens:tokens + 1, at], ctx_ref[tokens + 1:tokens + 2, at],
                    jnp.sum(turned[:half], axis=0, keepdims=True), jnp.sum(turned[half:], axis=0, keepdims=True)]
            pieces = []
            for value in rows:
                for _ in range(3):
                    piece = value.astype(bf16).astype(f32)
                    pieces.append(piece)
                    value = value - piece
            pieces.append(vectors[:, at])
            pay_ref[tokens:, at] = jnp.concatenate(pieces, axis=0).astype(bf16)
        if part_ref is not None:
            pack(part_ref, 0, turn_ref, turn_ref.shape[0], 1, cols)


def layer_backward(pair, slope, down, up, d_h2, unit, scaled, gain1, out_weight, ctx, vec, cols, dealt):
    tokens, width = d_h2.shape
    units = up.shape[1]
    chunk = width
    square = (tokens, width)
    shapes = [(square, f32), ((tokens + EXTRA, width), bf16), ((tokens, units), bf16)]
    specs = [full(square), full((tokens + EXTRA, width)), step_cols(tokens, chunk)]
    kernel = functools.partial(layer_backward_kernel, cols)
    if dealt:
        shapes.append(((cols, units // cols, tokens), bf16))
        specs.append(full(shapes[-1][0]))
    else:
        kernel = lambda *refs: layer_backward_kernel(cols, *refs[:-2], None, *refs[-2:])
    return pl.pallas_call(
        kernel,
        grid=(units // chunk,),
        in_specs=[full((tokens, 2 * width)), step_cols(tokens, chunk), step_rows(chunk, width), step_cols(width, chunk),
                  full(square), full(square), full((tokens, PAIR)), full((1, width)), full(out_weight.shape), full(ctx.shape),
                  full((8, width))],
        out_specs=specs,
        out_shape=[jax.ShapeDtypeStruct(*x) for x in shapes],
        scratch_shapes=[pltpu.VMEM(square, f32), pltpu.VMEM((units, tokens), f32)],
        compiler_params=params(),
        cost_estimate=cost(1),
        name="layer_backward",
    )(pair, slope, down, up, d_h2, unit, scaled, gain1.reshape(1, width), out_weight, ctx, vec)


def layer_sums_kernel(rows, chunk, place_ref, pair_even_ref, pair_odd_ref, mine_ref, twin_ref, even_ref, odd_ref, act_ref,
                      din_ref, earlier_ref, *out_refs):
    *out_refs, out_ref = out_refs
    me = 2 * place_ref[0] + place_ref[1]
    width = mine_ref.shape[1]
    features = act_ref.shape[1] - chunk
    half = width // 2
    down = up = out = small = 0.0
    for i in range(act_ref.shape[0] // 2):
        part = lanes([act_ref[me ^ (2 * i)], act_ref[me ^ (2 * i + 1)]])
        din = lanes([din_ref[me ^ (2 * i)], din_ref[me ^ (2 * i + 1)]])
        normed = jnp.concatenate([pair_even_ref[i, :, :width], pair_odd_ref[i, :, :width]], axis=0)
        branch = jnp.concatenate([pair_even_ref[i, :, width:], pair_odd_ref[i, :, width:]], axis=0)
        first, second = (even_ref.at[i - 1], odd_ref.at[i - 1]) if i else (mine_ref, twin_ref)
        attn = jnp.concatenate([first[:TOK, :], second[:TOK, :]], axis=0)
        down = down + dot(part[:chunk], branch, NN)
        out = out + dot(part[chunk:], attn, NN)
        up = up + dot(din, normed, NN)
        small = small + first[TOK:, :].astype(f32) + second[TOK:, :].astype(f32)
    up = up.T
    small = small[EXTRA - 4:]
    share, size, few = width // rows, chunk // rows, features // rows
    for r in range(rows):
        vectors = lanes([small[:, r * share:(r + 1) * share], jnp.zeros((4, chunk - share), f32)])
        pieces = [
            down[r * size:(r + 1) * size, :half], down[r * size:(r + 1) * size, half:],
            up[r * share:(r + 1) * share],
            out[r * few:(r + 1) * few, :half], out[r * few:(r + 1) * few, half:],
            vectors, jnp.zeros((EXTRA - 4, chunk), f32),
        ]
        out_ref[r] = jnp.concatenate(pieces, axis=0).astype(bf16)
    for k, ref in enumerate(out_refs):
        ref[...] = out_ref[place_ref[2] ^ k]


def layer_sums(place, pair, attn, act, din, earlier, rows, chunk):
    width = attn[0].shape[1]
    features = act.shape[1] - chunk
    height = (2 * chunk + 2 * features) // rows + width // rows + EXTRA
    return pl.pallas_call(
        functools.partial(layer_sums_kernel, rows, chunk),
        in_specs=[scalar()] + [whole()] * 8 + [unread()],
        out_specs=[whole()] * rows,
        out_shape=[jax.ShapeDtypeStruct((height, chunk), bf16)] * rows,
        scratch_shapes=[pltpu.VMEM((rows, height, chunk), bf16)],
        compiler_params=params(),
        cost_estimate=cost(6),
        name="layer_sums",
    )(place, *pair, *attn, act, din, earlier)


def layer_unpack_kernel(cols, place_ref, even_ref, odd_ref, down_ref, up_ref, out_ref, small_ref):
    me = 2 * place_ref[0] + place_ref[1]
    half = down_ref.shape[1] // 2
    size, share, few = down_ref.shape[0] // cols, up_ref.shape[0], out_ref.shape[0] // cols
    chunk = up_ref.shape[1] // cols
    for ref, odd in ((even_ref, 0), (odd_ref, 1)):
        for i in range(cols // 2):
            spot = me ^ (2 * i + odd)
            part = ref[i].astype(f32)
            down_rows = pl.ds(pl.multiple_of(spot * size, 8), size)
            down_ref[down_rows, :half] = part[:size]
            down_ref[down_rows, half:] = part[size:2 * size]
            at = 2 * size + share
            up_ref[:, pl.ds(pl.multiple_of(spot * chunk, PAIR), chunk)] = part[2 * size:at]
            out_rows = pl.ds(pl.multiple_of(spot * few, 8), few)
            out_ref[out_rows, :half] = part[at:at + few]
            out_ref[out_rows, half:] = part[at + few:at + 2 * few]
            if i == 0 and not odd:
                small_ref[...] = part[at + 2 * few:at + 2 * few + 8, :share]


def layer_unpack(place, even, odd, rows, width, units):
    cols = 2 * even.shape[0]
    share = width // rows
    shapes = [(units // rows, width), (share, units), (share, width), (8, share)]
    return pl.pallas_call(
        functools.partial(layer_unpack_kernel, cols),
        in_specs=[scalar()] + [whole()] * 2,
        out_specs=[whole()] * 4,
        out_shape=[jax.ShapeDtypeStruct(x, f32) for x in shapes],
        compiler_params=params(),
        cost_estimate=cost(4),
        name="layer_unpack",
    )(place, even, odd)


def attn_sums_kernel(rows, place_ref, rows_ref, rel_ref, *refs):
    *out_refs, out_ref = refs[-rows - 1:]
    refs = refs[:-rows - 2]
    count = len(refs) // 2
    size = refs[0].shape[0]
    width, places = rows_ref.shape[1], rel_ref.shape[0]
    table_q = table_k = query = key = value = 0.0
    for j in range(count):
        rows_in = rows_ref[j * BLK:(j + 1) * BLK, :]
        q_ref, k_ref = refs[j], refs[count + j]
        query = query + dot(q_ref[:, places:], rows_in, NN)
        key = key + dot(k_ref[:, places:places + BLK], rows_in, NN)
        value = value + dot(k_ref[:, places + BLK:], rows_in, NN)
        table_k = table_k + q_ref[:, :places].astype(f32)
        table_q = table_q + k_ref[:, :places].astype(f32)
    query = query + dot(table_q.astype(bf16), rel_ref[...], NN)
    key = key + dot(table_k.astype(bf16), rel_ref[...], NN)
    pieces = [query, key, value]
    fill = -3 * size % PAIR
    if fill:
        pieces.append(jnp.zeros((fill, width), f32))
    full_sum = jnp.concatenate(pieces, axis=0).T
    share, spots = width // rows, places // rows
    wide = full_sum.shape[1]
    both = jnp.concatenate([table_q, table_k], axis=0)
    lines = 2 * size * spots // wide
    for r in range(rows):
        cut = both[:, r * spots:(r + 1) * spots]
        cut = lanes([cut[j * lines:(j + 1) * lines] for j in range(wide // spots)])
        out_ref[r] = jnp.concatenate([full_sum[r * share:(r + 1) * share], cut], axis=0).astype(bf16)
    for k, ref in enumerate(out_refs):
        ref[...] = out_ref[place_ref[2] ^ k]


def attn_sums(place, rows_in, rel, q_parts, k_parts, earlier, rows):
    size = q_parts[0].shape[0]
    width, places = rows_in.shape[1], rel.shape[0]
    wide = 3 * size + (-3 * size % PAIR)
    height = width // rows + 2 * size * (places // rows) // wide
    return pl.pallas_call(
        functools.partial(attn_sums_kernel, rows),
        in_specs=[scalar()] + [whole()] * (2 + len(q_parts) + len(k_parts)) + [unread()],
        out_specs=[whole()] * rows,
        out_shape=[jax.ShapeDtypeStruct((height, wide), bf16)] * rows,
        scratch_shapes=[pltpu.VMEM((rows, height, wide), bf16)],
        compiler_params=params(),
        cost_estimate=cost(5),
        name="attn_sums",
    )(place, rows_in, rel, *q_parts, *k_parts, earlier)


def rel_kernel(cols, share, spots, place_ref, even_ref, odd_ref, wq_ref, wk_ref, rel_ref, tq_ref, tk_ref):
    me = 2 * place_ref[0] + place_ref[1]
    width = wq_ref.shape[0]
    size = width // cols
    for ref, odd in ((even_ref, 0), (odd_ref, 1)):
        for i in range(cols // 2):
            spot = me ^ (2 * i + odd)
            tail = ref[i, share:, :].astype(f32)
            tail = jnp.concatenate([tail[:, j * spots:(j + 1) * spots] for j in range(tail.shape[1] // spots)], axis=0)
            at = pl.ds(pl.multiple_of((spot % 2) * (width // 2) + (spot // 2) * size, EXTRA), size)
            tq_ref[at, :] = tail[:size].astype(bf16)
            tk_ref[at, :] = tail[size:].astype(bf16)
    flip = flip_matrix(spots)
    across = (((0,), (1,)), ((), ()))
    turned_q = dot(tq_ref[...], flip, NN).astype(bf16)
    turned_k = dot(tk_ref[...], flip, NN).astype(bf16)
    rel_ref[...] = (dot(turned_q, wq_ref[...], across) + dot(turned_k, wk_ref[...], across)).astype(bf16)


def rel_share(place, even, odd, wq, wk, rows, places):
    cols = 2 * even.shape[0]
    width = wq.shape[0]
    spots = places // rows
    return pl.pallas_call(
        functools.partial(rel_kernel, cols, width // rows, spots),
        in_specs=[scalar()] + [whole()] * 4,
        out_specs=whole(),
        out_shape=jax.ShapeDtypeStruct((spots, width), bf16),
        scratch_shapes=[pltpu.VMEM((width, spots), bf16)] * 2,
        compiler_params=params(),
        cost_estimate=cost(2),
        name="rel_share",
    )(place, even, odd, wq, wk)


def attn_unpack_kernel(cols, place_ref, even_ref, odd_ref, earlier_ref, q_ref, k_ref, v_ref, all_ref):
    me = 2 * place_ref[0] + place_ref[1]
    share, width = q_ref.shape
    size = width // cols
    for ref, odd in ((even_ref, 0), (odd_ref, 1)):
        for i in range(cols // 2):
            all_ref[me ^ (2 * i + odd)] = ref[i, :share, :].astype(f32)
    for c in range(cols):
        start = (c % 2) * width // 2 + (c // 2) * size
        for i, ref in enumerate((q_ref, k_ref, v_ref)):
            ref[:, start:start + size] = all_ref[c, :, i * size:(i + 1) * size]


def attn_unpack(place, even, odd, earlier, rows, width):
    count, _, wide = even.shape
    share = width // rows
    return pl.pallas_call(
        functools.partial(attn_unpack_kernel, 2 * count),
        in_specs=[scalar()] + [whole()] * 2 + [unread()],
        out_specs=[whole()] * 3,
        out_shape=[jax.ShapeDtypeStruct((share, width), f32)] * 3,
        scratch_shapes=[pltpu.VMEM((2 * count, share, wide), f32)],
        compiler_params=params(),
        cost_estimate=cost(4),
        name="attn_unpack",
    )(place, even, odd, earlier)


HEADS = 12


def mul(a, b, form=NN):
    return lax.dot_general(a, b, form, preferred_element_type=f32)


def swap(x, axis, k):
    return lax.ppermute(x, axis, [(i, i ^ k) for i in range(lax.axis_size(axis))])


def gather(x, *earlier):
    even = stack([x] + [swap(x, "seq", k) for k in range(2, lax.axis_size("seq"), 2)], *earlier)
    return even, swap(even, "seq", 1)


def gather_parts(x, *earlier):
    twin = swap(x, "seq", 1)
    even = stack([swap(x, "seq", k) for k in range(2, lax.axis_size("seq"), 2)], *earlier)
    return x, twin, even, swap(even, "seq", 1)


def deal_rows(parts, *earlier):
    return sum_arrays([swap(part, "row", k) if k else part for k, part in enumerate(parts)], *earlier)


def deal_chips(parts):
    return [parts[0]] + [swap(part, "seq", 2 * k) for k, part in enumerate(parts) if k]


def in_order(parts, chip):
    out = jnp.zeros((len(parts),) + parts[0].shape, parts[0].dtype)
    for k, part in enumerate(parts):
        out = lax.dynamic_update_slice_in_dim(out, part[None], chip ^ k, 0)
    return out.reshape((-1,) + parts[0].shape[1:])


def reduced(g):
    part = lax.psum_scatter(g.astype(bf16), "row", scatter_dimension=0, tiled=True)
    return lax.psum(part, "seq").astype(f32)


def on_device(
    hidden, segments, rel_embed, query_weight, key_weight, value_weight, output_weight, up_weight, down_weight,
    norm1_gain, norm1_bias, norm2_gain, norm2_bias, cotangent,
):
    tokens, width = hidden.shape[1:]
    places = rel_embed.shape[0]
    units = up_weight.shape[1]
    part = width // 2
    scale = 1.0 / math.sqrt(3.0 * (width // HEADS))
    inputs = hidden[0]
    cols, rows = lax.axis_size("seq"), lax.axis_size("row")
    chip, core = lax.axis_index("seq") // 2, lax.axis_index("seq") % 2
    row = lax.axis_index("row")
    place = jnp.stack([chip, core, row]).astype(jnp.int32)
    share = width // rows
    chunk = units // cols
    dealt = (units // (rows * cols)) % 16 == 0 and places // rows == TOK

    def core_cols(w):
        return lax.dynamic_slice_in_dim(w, core * part, part, 1)

    def meet(x):
        mine = lax.dynamic_index_in_dim(x, core, 0, keepdims=False)
        other = swap(lax.dynamic_index_in_dim(x, 1 - core, 0, keepdims=False), "seq", 1)
        return jnp.where(core == 0, jnp.concatenate([mine, other], axis=-1), jnp.concatenate([other, mine], axis=-1))

    half_q, half_k, half_v = core_cols(query_weight), core_cols(key_weight), core_cols(value_weight)
    half_out = lax.dynamic_slice_in_dim(output_weight, core * part, part, 0)
    rel_flip = mul(flip_matrix(places), rel_embed).astype(bf16)
    qr = mul(rel_flip, half_q).astype(bf16)
    kr = mul(rel_flip, half_k).astype(bf16)
    seg_rows = jnp.pad(segments.astype(bf16), ((0, EXTRA - 1), (0, width - tokens)))
    in_parts = gather_parts(jnp.concatenate([inputs, seg_rows], axis=0), qr, kr)
    q, k, v, row_segs, row_in = project_rows(place, in_parts, half_q, half_k, half_v)
    own_segs = row_segs[0, :BLK].reshape(BLK, 1)

    probs, ctx_half = forward_attention(place, q, k, v, kr, qr, own_segs, row_segs, scale)
    ctx = meet(ctx_half)

    norms = (norm1_gain, norm1_bias, norm2_gain, norm2_bias)
    output, pair_low, active_low, slope, unit1, scaled1, d_h2, vec, *act = layer_forward(
        inputs, ctx, output_weight, up_weight, down_weight, cotangent[0], norms, cols, rows, dealt
    )
    d_h1, attn_pay, d_inner, *parts = layer_backward(
        pair_low, slope, down_weight, up_weight, d_h2, unit1, scaled1, norm1_gain, output_weight, ctx, vec, cols, dealt
    )
    if dealt:
        act, = (lax.all_to_all(x, "seq", 0, 0, tiled=True) for x in act)

        parts, = parts
        parts = lax.all_to_all(after(parts, act), "seq", 0, 0, tiled=True)
    else:
        act = parts = attn_pay
    twin = swap(attn_pay, "seq", 1)
    dq_half, *q_table = query_grads(place, probs, attn_pay, twin, half_out, ctx_half, v, q, k, kr, act, scale)
    even = stack([swap(attn_pay, "seq", i) for i in range(2, cols, 2)], dq_half)
    attn = attn_pay, twin, even, swap(even, "seq", 1)
    if dealt:
        q_parts = deal_chips(q_table)
        pair = gather(pair_low, dq_half)
        layer_part = layer_sums(place, pair, attn, act, parts, dq_half, rows, chunk)
    dk_half, dv_half, *k_table = key_grads(
        place, k, v, q, qr, kr, own_segs, row_segs, attn, half_out, after(layer_part[0], *q_parts[1:]) if dealt else act, scale
    )
    d_own = meet(jnp.concatenate([dq_half, dk_half, dv_half], axis=1))
    dq, dk, dv = (d_own[i * tokens:(i + 1) * tokens] for i in range(3))
    grad_in = d_h1 + mul(dq, query_weight, NT) + mul(dk, key_weight, NT) + mul(dv, value_weight, NT)
    grad_in = grad_in.astype(bf16)

    if dealt:
        k_parts = deal_chips(k_table)
        layer = deal_rows(layer_part, dk_half)
        attn_part = attn_sums(place, row_in, rel_flip, q_parts, k_parts, layer, rows)
        attn_sum = deal_rows(attn_part)
        g_down, g_up, g_output, small = layer_unpack(place, *gather(after(layer, attn_part[0]), attn_sum), rows, width, units)
        sums = gather(attn_sum)
        g_rel = rel_share(place, *sums, query_weight, key_weight, rows, places)
        g_query, g_key, g_value = attn_unpack(place, *sums, g_rel, rows, width)
        g_rel = join_rows(place, [g_rel] + [swap(g_rel, "row", k) for k in range(1, rows)], small, grad_in)
    else:
        small = jnp.stack([reduced(x) for x in attn_pay[tokens + EXTRA - 4:]])
        g_down = reduced(mul(active_low, pair_low[:, width:], TN))
        g_up = reduced(mul(pair_low[:, :width], d_inner, TN))
        g_output = reduced(mul(ctx[:tokens].astype(bf16), attn_pay[:tokens], TN))
        across = (((0,), (1,)), ((), ()))
        d_kr, d_qr = (in_order(x, chip)[:, :places] for x in (q_table, k_table))
        placed = lambda g: lax.dynamic_update_slice_in_dim(jnp.zeros((width, width), f32), g, core * part, 1)
        g_query = reduced(mul(inputs, dq, TN) + placed(mul(rel_flip, d_qr, across)))
        g_key = reduced(mul(inputs, dk, TN) + placed(mul(rel_flip, d_kr, across)))
        g_value = reduced(mul(inputs, dv, TN))
        g_rel = mul(d_qr, half_q, across) + mul(d_kr, half_k, across)
        g_rel = lax.psum(mul(flip_matrix(places), g_rel.astype(bf16)).astype(bf16), ("seq", "row")).astype(f32)

    return (
        output[None], grad_in[None], g_query, g_key, g_value, g_output, g_up, g_down,
        small[0], small[1], small[2], small[3], g_rel,
    )


def solution(mesh):
    split = P("row", "seq", None)
    return jax.shard_map(
        on_device,
        mesh=mesh,
        in_specs=(split, P("row", "seq")) + (P(),) * 11 + (split,),
        out_specs=(split, split) + (P("row", None),) * 6 + (P("row"),) * 4 + (P(),),
        check_vma=False,
    )
```
